512 devices in a mesh: scan: 32 (over y, z_lo, core), det: 16 (over x, z_hi).
Axes of the slice: x: 4, y: 4, z: 16 (z_hi: 4, z_lo: 4; z = z_hi * 4 + z_lo), core: 2. Of those that a mesh axis runs over, the one named last changes fastest.
Arguments:
- intensities: float32 [64, 1024, 1024], P('det', 'scan'), may hold values from -6 to 6
- trotter_labels: int32 [64, 1024, 1024], P('det', 'scan'), may hold values from 0 to 2
- phase_shift: float32 [1024, 1024], P('scan'), may hold values from -3.140625 to 3.140625
Outputs:
- object_spectrum: float32 [2, 1024, 1024], P(None, 'scan', 'det')
The draws below stay inside these ranges and needn't reach their ends.
Inputs may be any that keep to these rules, and one draw needn't show every extreme that they name: `trotter_labels`: 0: the pixel lies in neither aperture margin at that frequency; 1: in the left margin; 2: in the right margin.
All inputs are finite; a program needn't handle non-finite values.
Results may differ from the reference program's by a relative error of at most 0.0003.
Values sent between devices are 32-bit elements; how exact they have to be, the bound alone decides.
A program may use at most 64 MiB of HBM per device.

```python
import math
import jax
import jax.numpy as jnp
from jax import lax

NR = 1024
NC = 1024
PIXELS = 64


def place_ends(result, key, least, largest):
    longest = result.shape.index(max(result.shape))
    spots = []
    for shift in (0, 1):
        where = [jax.random.randint(jax.random.fold_in(key, axis), (), 0, length) for axis, length in enumerate(result.shape)]
        where[longest] = (where[longest] + shift) % result.shape[longest]
        spots.append(tuple(where))
    return result.at[spots[0]].set(least).at[spots[1]].set(largest)


def block_scale(rng, shape, cuts, low, largest):
    level = 1.0
    for position, shards_of in cuts:
        heights = jax.random.uniform(jax.random.fold_in(jax.random.fold_in(rng, 6), position), (shards_of,), jnp.float32, low / len(cuts), largest / len(cuts))
        level = level * jnp.repeat(jnp.exp(heights), shape[position] // shards_of).reshape((-1,) + (1,) * (len(shape) - 1 - position))
    return level


def bell_draw(stream_key, extent, spread, bound, split=(), kind=jnp.bfloat16):
    drawn = spread * jax.random.normal(stream_key, extent, jnp.float32)
    if split:
        drawn = drawn * block_scale(stream_key, extent, split, -0.22, 0.18)
    return jnp.clip(drawn, -bound, bound).astype(kind)


def setup_inputs(seed: int = 0) -> dict:
    arg_keys = jax.random.split(jax.random.key(seed), 4)
    return {
        "intensities": bell_draw(arg_keys[0], (PIXELS, NR, NC), 1.0, 6.0, ((0, 16), (1, 32)), jnp.float32),
        "trotter_labels": place_ends(jax.random.randint(arg_keys[1], (PIXELS, NC, NR), 0, 3), jax.random.fold_in(arg_keys[1], 1), 0, 2).astype(jnp.int32),
        "phase_shift": jnp.clip(jax.random.uniform(arg_keys[2], (NC, NR), jnp.float32, -3.140625, 3.140625), -3.140625, 3.140625),
    }


def weights_of(labels, phase):
    cosine = jnp.cos(phase)
    sine_part = jnp.sin(phase)
    left_side = labels == 1
    right_side = labels == 2
    either = jnp.logical_or(left_side, right_side)
    empty_part = jnp.zeros_like(cosine)
    weight_real = jnp.where(left_side, cosine, jnp.where(right_side, -cosine, empty_part))
    weight_imag = jnp.where(either, -sine_part, empty_part)
    return (weight_real, weight_imag)

def reference(intensities, trotter_labels, phase_shift):
    normalizer = 1.0 / math.sqrt(NR * NC)

    def accumulate(totals, pieces):
        frame_data, labels = pieces
        spectrum = jnp.fft.fft2(frame_data)
        spec_real = jnp.real(spectrum).T * normalizer
        spec_imag = jnp.imag(spectrum).T * normalizer
        weight_real, weight_imag = weights_of(labels, phase_shift)
        new_real = totals[0] + spec_real * weight_real - spec_imag * weight_imag
        new_imag = totals[1] + spec_real * weight_imag + spec_imag * weight_real
        return ((new_real, new_imag), None)
    empty_sum = jnp.zeros((NC, NR), jnp.float32)
    (total_real, total_imag), ignored = lax.scan(accumulate, (empty_sum, empty_sum), (intensities, trotter_labels))
    return jnp.stack([total_real, total_imag]) / math.sqrt(PIXELS)
```

```python
import math

import jax
import jax.numpy as jnp
import ml_dtypes
import numpy as np
from jax import lax
from jax.experimental import pallas as pl
from jax.experimental.pallas import tpu as pltpu
from jax.sharding import PartitionSpec as P

MESH = pl.DeviceIdType.MESH
F32 = jnp.float32
BF16 = jnp.bfloat16

N = 1024
SCAN = 32
BLOCK = 32
PARTS = (0, 2, 1, 3)
ROWS = BLOCK // 4
PIX = 4
X = 4
Z = 4


def split_table(table):
    high = table.astype(ml_dtypes.bfloat16)
    low = (table - high.astype(np.float64)).astype(ml_dtypes.bfloat16)
    return high, low


def make_tables():
    index = np.arange(N)
    angles = (index[:, None] * index[None, :] % N) * (2.0 * math.pi / N)
    cosine, sine = np.cos(angles), np.sin(angles)
    cos_v = cosine[:, :256].reshape(SCAN, ROWS, 4, 256)
    sin_v = sine[:, :256].reshape(SCAN, ROWS, 4, 256)
    even, odd = [], []
    for v in PARTS:
        c, s = cos_v[:, :, v], sin_v[:, :, v]
        if v % 2 == 0:
            table = np.stack([c, -s], axis=1)
        else:
            sign = 1.0 if v == 3 else -1.0
            table = np.stack(
                [np.concatenate([c, sign * s], 2), np.concatenate([-s, sign * c], 2)], axis=1)
        table = np.concatenate(split_table(table.reshape(512, -1)), axis=0)
        (odd if v % 2 else even).append(table)
    twiddle = np.stack([cosine[:32, :32], sine[:32, :32]])
    twiddle = np.tile(twiddle, (1, 1, PIX)).astype(np.float32)[:, :, None]
    twiddle = np.repeat(twiddle, ROWS, axis=2)
    u2 = np.arange(32)
    lanes = ((u2 % 4) * 32 + u2 // 4)[None, :] + 8 * np.arange(PIX)[:, None]
    small = np.zeros((2, 128, 128))
    for k in range(PIX):
        for e, table in enumerate((cosine, sine)):
            small[e, k * 32:(k + 1) * 32, lanes[k]] = table[:32, 0:N:32].T
    row = np.block([[small[0], -small[1]], [small[1], small[0]]]) / (N * 8.0)
    row = np.stack(split_table(row))
    return np.stack(even), np.stack(odd), row, twiddle


def swap_bit(first, second, width):
    clear = lax.broadcasted_iota(jnp.int32, first.shape, 1) % (2 * width) < width
    return (
        jnp.where(clear, first, pltpu.roll(second, width, 1)),
        jnp.where(clear, pltpu.roll(first, 128 - width, 1), second),
    )


def swap_bits(parts, widths):
    parts = list(parts)
    step = len(parts)
    for width in widths:
        step //= 2
        for n in range(len(parts)):
            if n // step % 2 == 0:
                parts[n], parts[n + step] = swap_bit(parts[n], parts[n + step], width)
    return parts


def sum_blocks(parts):
    lane = lax.broadcasted_iota(jnp.int32, parts[0].shape, 1)
    for width in (16, 8):
        clear = lane % (2 * width) < width
        half = len(parts) // 2
        sums = []
        for one, two in zip(parts[:half], parts[half:]):
            other = jnp.where(clear, two, one)
            other = jnp.where(
                clear, pltpu.roll(other, 128 - width, 1), pltpu.roll(other, width, 1))
            sums.append(jnp.where(clear, one, two) + other)
        parts = sums
    return parts[0]


def four_points(p):
    (ar, ai), (br, bi), (cr, ci), (dr, di) = p
    sr, si, er, ei = ar + cr, ai + ci, ar - cr, ai - ci
    tr, ti, fr, fi = br + dr, bi + di, br - dr, bi - di
    return [(sr + tr, si + ti), (er + fi, ei - fr), (sr - tr, si - ti), (er - fi, ei + fr)]


def eight_points(p):
    root = math.sqrt(0.5)
    even = four_points(p[0::2])
    odd = four_points(p[1::2])
    (r1, i1), (r2, i2), (r3, i3) = odd[1:]
    odd[1] = ((r1 + i1) * root, (i1 - r1) * root)
    odd[2] = (i2, -r2)
    odd[3] = ((i3 - r3) * root, -(r3 + i3) * root)
    out = [(e[0] + o[0], e[1] + o[1]) for e, o in zip(even, odd)]
    return out + [(e[0] - o[0], e[1] - o[1]) for e, o in zip(even, odd)]


def turn(p, step):
    if step == 0:
        return p
    c, s = math.cos(2.0 * math.pi * step / 32), math.sin(2.0 * math.pi * step / 32)
    return p[0] * c + p[1] * s, p[1] * c - p[0] * s


def split3(value):
    high = value.astype(BF16)
    rest = value - high.astype(F32)
    middle = rest.astype(BF16)
    return high, middle, (rest - middle.astype(F32)).astype(BF16)


def kernel(
    x_hbm, lab_hbm, phase_hbm, even_hbm, odd_hbm, row_hbm, twiddle_hbm, o_ref,
    x_v, lab_v, phase_v, even_v, odd_v, row_v, twiddle_v,
    xt, sbuf, rbuf, mixed, turned, lhs, cos_v, sin_v,
    wr, wi, psend, precv, zsend, zrecv, o_v,
    in_sem, send_sem, recv_sem, psend_sem, precv_sem, zsend_sem, zrecv_sem,
):
    me = lax.axis_index("scan")
    det = lax.axis_index("det")
    x, z = det // Z, det % Z

    x_copy = pltpu.make_async_copy(x_hbm, x_v, in_sem.at[0])
    lab_copies = [
        pltpu.make_async_copy(
            lab_hbm.at[:, :, pl.ds(m * 128, 128)], lab_v.at[m], in_sem.at[1])
        for m in range(8)
    ]
    phase_copies = [
        pltpu.make_async_copy(phase_hbm.at[:, pl.ds(m * 128, 128)], phase_v.at[m], in_sem.at[2])
        for m in range(8)
    ]
    row_copy = pltpu.make_async_copy(row_hbm, row_v, in_sem.at[3])
    twiddle_copy = pltpu.make_async_copy(twiddle_hbm, twiddle_v, in_sem.at[4])
    col_copies = [
        pltpu.make_async_copy(table.at[p % 2], to.at[p % 2], in_sem.at[6 + p])
        for p, (table, to) in enumerate([(even_hbm, even_v)] * 2 + [(odd_hbm, odd_v)] * 2)
    ]

    x_copy.start()
    col_copies[0].start()

    barrier = pltpu.get_barrier_semaphore()

    @pl.loop(1, SCAN)
    def _(i):
        pl.semaphore_signal(
            barrier, inc=1, device_id=(lax.rem(me + i, SCAN), det), device_id_type=MESH)

    for i in range(1, 4):
        pl.semaphore_signal(
            barrier, inc=1, device_id=(me, lax.rem(x + i, X) * Z + z), device_id_type=MESH)
        pl.semaphore_signal(
            barrier, inc=1, device_id=(me, x * Z + lax.rem(z + i, Z)), device_id_type=MESH)

    for p in range(1, 4):
        col_copies[p].start()
    for copy in lab_copies + phase_copies:
        copy.start()
    row_copy.start()
    twiddle_copy.start()

    x_copy.wait()
    quarter = [[x_v[:, :, q * 256 + h * 128:q * 256 + (h + 1) * 128].reshape(128, 128)
                for q in range(4)] for h in range(2)]

    def put(value, at):
        value = jnp.transpose(value)
        high = value.astype(BF16)
        xt[at:at + 128, :128] = high
        xt[at:at + 128, 128:] = (value - high.astype(F32)).astype(BF16)

    for h, (x0, x1, x2, x3) in enumerate(quarter):
        put((x0 + x2) + (x1 + x3), h * 128)

    def column_part(p):
        col_copies[p].wait()
        table = even_v if p < 2 else odd_v
        rows = xt[p * 256:(p + 1) * 256] if p < 2 else xt[512:]
        prod = jnp.dot(table[p % 2], rows, preferred_element_type=F32)
        top = prod[:512] + prod[512:]
        sbuf[p] = (top[:, :128] + top[:, 128:]).reshape(SCAN, 2, ROWS, 128)

    column_part(0)
    for h, (x0, x1, x2, x3) in enumerate(quarter):
        put((x0 + x2) - (x1 + x3), 256 + h * 128)
    column_part(1)
    for h, (x0, x1, x2, x3) in enumerate(quarter):
        put(x0 - x2, 512 + h * 128)
        put(x1 - x3, 768 + h * 128)
    column_part(2)
    column_part(3)

    pl.semaphore_wait(barrier, SCAN - 1 + X - 1 + Z - 1)
    chip = lax.div(me, 2)

    @pl.loop(0, 8)
    def _(n):
        p, core = lax.div(n, 2), lax.rem(n, 2)

        @pl.loop(1, 17)
        def _(i):
            to = lax.rem(chip + i, 16) * 2 + core

            @pl.when(to != me)
            def _():
                pltpu.make_async_remote_copy(
                    src_ref=sbuf.at[p, to],
                    dst_ref=rbuf.at[p, me],
                    send_sem=send_sem,
                    recv_sem=recv_sem.at[p],
                    device_id=(to, det),
                    device_id_type=MESH,
                ).start()

    for p in range(4):
        rbuf[p, me] = sbuf[p, me]

    pltpu.make_async_copy(phase_v, phase_v, in_sem.at[2]).wait()
    cos_v[...] = jnp.cos(phase_v[...])
    sin_v[...] = jnp.sin(phase_v[...])
    pltpu.make_async_copy(lab_v, lab_v, in_sem.at[1]).wait()
    for p, v in enumerate(PARTS):
        reals, imags = [], []
        for k in range(PIX):
            for m in range(8):
                cosine = cos_v[m, pl.ds(v, ROWS, stride=4), :]
                sine = sin_v[m, pl.ds(v, ROWS, stride=4), :]
                zero = jnp.zeros_like(cosine)
                labels = lab_v[m, k, pl.ds(v, ROWS, stride=4), :]
                left = labels == 1
                right = labels == 2
                reals.append(jnp.where(left, cosine, jnp.where(right, -cosine, zero)))
                imags.append(jnp.where(jnp.logical_or(left, right), -sine, zero))
        for to, parts in ((wr, reals), (wi, imags)):
            for u1, part in enumerate(swap_bits(parts, (16, 8, 4, 2, 1))):
                to[p, u1] = part

    row_copy.wait()
    twiddle_copy.wait()

    def row_part(p):
        most = rbuf.at[p, pl.ds(0, SCAN - 1)]
        pltpu.make_async_copy(most, most, recv_sem.at[p]).wait()
        for e in range(4):
            points = [(rbuf[p, 4 * g + e, 0], rbuf[p, 4 * g + e, 1]) for g in range(8)]
            for b, point in enumerate(eight_points(points)):
                mixed[e, b, 0], mixed[e, b, 1] = turn(point, e * b)
        for b in range(8):
            points = four_points([(mixed[e, b, 0], mixed[e, b, 1]) for e in range(4)])
            for c, (re, im) in enumerate(points):
                u1 = b + 8 * c
                cosine, sine = twiddle_v[0, u1], twiddle_v[1, u1]
                turned[u1 * ROWS:(u1 + 1) * ROWS, :128] = re * cosine + im * sine
                turned[u1 * ROWS:(u1 + 1) * ROWS, 128:] = im * cosine - re * sine
        for qh in range(2):
            value = turned[qh * 128:(qh + 1) * 128]
            high = value.astype(BF16)
            lhs[qh, :128] = high
            lhs[qh, 128:] = (value - high.astype(F32)).astype(BF16)
            both = jnp.dot(lhs[qh], row_v[0], preferred_element_type=F32)
            low = jnp.dot(lhs[qh, :128], row_v[1], preferred_element_type=F32)
            spec = both[:128] + both[128:] + low
            sums = [], []
            for ql in range(4):
                reals, imags = [], []
                for e in range(4):
                    at = ql * 4 + e
                    re = spec[at * ROWS:(at + 1) * ROWS, :128]
                    im = spec[at * ROWS:(at + 1) * ROWS, 128:]
                    w_re, w_im = wr[p, qh * 16 + at], wi[p, qh * 16 + at]
                    reals.append(re * w_re - im * w_im)
                    imags.append(re * w_im + im * w_re)
                sums[0].append(sum_blocks(reals))
                sums[1].append(sum_blocks(imags))
            for e in range(2):
                for q, part in enumerate(swap_bits(sums[e], (4, 2))):
                    psend[p, q, qh, e] = part

        @pl.loop(1, X)
        def _(j):
            q = (x + j) % X
            pltpu.make_async_remote_copy(
                src_ref=psend.at[p, q],
                dst_ref=precv.at[p, j - 1],
                send_sem=psend_sem.at[p],
                recv_sem=precv_sem.at[p],
                device_id=(me, q * Z + z),
                device_id_type=MESH,
            ).start()

    def sum_x(p):
        pltpu.make_async_copy(precv.at[p], precv.at[p], precv_sem.at[p]).wait()
        parts = []
        for qh in range(2):
            for e in range(2):
                total = psend[p, x, qh, e]
                for j in range(X - 1):
                    total = total + precv[p, j, qh, e]
                parts.append(total)
        for h, part in enumerate(swap_bits(parts, (1, 64))):
            zsend[p, h] = part

        @pl.loop(1, Z)
        def _(j):
            to = (z + j) % Z
            pltpu.make_async_remote_copy(
                src_ref=zsend.at[p, to],
                dst_ref=zrecv.at[p, j - 1],
                send_sem=zsend_sem.at[p],
                recv_sem=zrecv_sem.at[p],
                device_id=(me, x * Z + to),
                device_id_type=MESH,
            ).start()

    @pl.loop(0, 4)
    def _(p):
        @pl.when(p > 0)
        def _():
            sum_x(p - 1)

        row_part(p)

    sum_x(3)

    lane = lax.broadcasted_iota(jnp.int32, (128, 128), 0)
    target = (
        lane // 32 * 32 + (lane % 2 * 4 + lane // 2 % 4) * 4 + lane // 8 % 4)
    order = jnp.where(
        target == lax.broadcasted_iota(jnp.int32, (128, 128), 1), 1.0, 0.0).astype(BF16)
    results = []
    for p in range(4):
        pltpu.make_async_copy(zrecv.at[p], zrecv.at[p], zrecv_sem.at[p]).wait()
        results.append(zsend[p, z] + zrecv[p, 0] + zrecv[p, 1] + zrecv[p, 2])
    result = jnp.concatenate(results, axis=0)
    moved = jnp.dot(jnp.concatenate(split3(result), axis=0), order, preferred_element_type=F32)
    result = moved[:BLOCK] + moved[BLOCK:2 * BLOCK] + moved[2 * BLOCK:]
    other = pltpu.roll(result, 64, 1)
    for p, v in enumerate(PARTS):
        o_v[0, pl.ds(v, ROWS, stride=4), :] = result[p * ROWS:(p + 1) * ROWS]
        o_v[1, pl.ds(v, ROWS, stride=4), :] = other[p * ROWS:(p + 1) * ROWS]
    o_ref[...] = o_v[:, :, :N // (X * Z)]

    for p in range(4):
        most = rbuf.at[p, pl.ds(0, SCAN - 1)]
        pltpu.make_async_copy(most, most, send_sem).wait()
        pltpu.make_async_copy(precv.at[p], precv.at[p], psend_sem.at[p]).wait()
        pltpu.make_async_copy(zrecv.at[p], zrecv.at[p], zsend_sem.at[p]).wait()


def local(even, odd, row, twiddle, intensities, trotter_labels, phase_shift):
    any_spec = pl.BlockSpec(memory_space=pl.ANY)
    dma = pltpu.SemaphoreType.DMA
    return pl.pallas_call(
        kernel,
        out_shape=jax.ShapeDtypeStruct((2, BLOCK, N // (X * Z)), F32),
        in_specs=[any_spec] * 7,
        out_specs=pl.BlockSpec(memory_space=pltpu.VMEM),
        scratch_shapes=[
            pltpu.VMEM((PIX, BLOCK, N), F32),
            pltpu.VMEM((8, PIX, BLOCK, 128), jnp.int32),
            pltpu.VMEM((8, BLOCK, 128), F32),
            pltpu.VMEM((2, 1024, 256), BF16),
            pltpu.VMEM((2, 1024, 512), BF16),
            pltpu.VMEM((2, 256, 256), BF16),
            pltpu.VMEM((2, 32, ROWS, 128), F32),
            pltpu.VMEM((N, 256), BF16),
            pltpu.VMEM((4, SCAN, 2, ROWS, 128), F32),
            pltpu.VMEM((4, SCAN, 2, ROWS, 128), F32),
            pltpu.VMEM((4, 8, 2, ROWS, 128), F32),
            pltpu.VMEM((256, 256), F32),
            pltpu.VMEM((2, 256, 256), BF16),
            pltpu.VMEM((8, BLOCK, 128), F32),
            pltpu.VMEM((8, BLOCK, 128), F32),
            pltpu.VMEM((4, 32, ROWS, 128), F32),
            pltpu.VMEM((4, 32, ROWS, 128), F32),
            pltpu.VMEM((4, X, 2, 2, ROWS, 128), F32),
            pltpu.VMEM((4, X - 1, 2, 2, ROWS, 128), F32),
            pltpu.VMEM((4, Z, ROWS, 128), F32),
            pltpu.VMEM((4, Z - 1, ROWS, 128), F32),
            pltpu.VMEM((2, BLOCK, 128), F32),
            dma((10,)),
            dma,
            dma((4,)),
            dma((4,)),
            dma((4,)),
            dma((4,)),
            dma((4,)),
        ],
        compiler_params=pltpu.CompilerParams(
            collective_id=0, has_side_effects=True, vmem_limit_bytes=55140 * 1024),
        name="ptycho",
    )(intensities, trotter_labels, phase_shift, even, odd, row, twiddle)


def solution(mesh):
    tables = make_tables()
    placed = (P("det", "scan", None), P("det", "scan", None), P("scan", None))
    fixed = tuple(P(*[None] * table.ndim) for table in tables)
    mapped = jax.shard_map(
        local, mesh=mesh, in_specs=fixed + placed, out_specs=P(None, "scan", "det"),
        check_vma=False)

    def run(intensities, trotter_labels, phase_shift):
        return mapped(*map(jnp.asarray, tables), intensities, trotter_labels, phase_shift)

    return run
```

```python
import math

import jax
import jax.numpy as jnp
import ml_dtypes
import numpy as np
from jax import lax
from jax.experimental import pallas as pl
from jax.experimental.pallas import tpu as pltpu
from jax.sharding import PartitionSpec as P

MESH = pl.DeviceIdType.MESH
F32 = jnp.float32
BF16 = jnp.bfloat16

N = 1024
SCAN = 32
BLOCK = 32
PARTS = (0, 2, 1, 3)
ROWS = BLOCK // 4
PIX = 4
X = 4
Z = 4


def split_table(table):
    high = table.astype(ml_dtypes.bfloat16)
    low = (table - high.astype(np.float64)).astype(ml_dtypes.bfloat16)
    return high, low


def make_tables():
    index = np.arange(N)
    angles = (index[:, None] * index[None, :] % N) * (2.0 * math.pi / N)
    cosine, sine = np.cos(angles), np.sin(angles)
    cos_v = cosine[:, :256].reshape(SCAN, ROWS, 4, 256)
    sin_v = sine[:, :256].reshape(SCAN, ROWS, 4, 256)
    even, odd = [], []
    for v in PARTS:
        c, s = cos_v[:, :, v], sin_v[:, :, v]
        if v % 2 == 0:
            table = np.stack([c, -s], axis=1)
        else:
            sign = 1.0 if v == 3 else -1.0
            table = np.stack(
                [np.concatenate([c, sign * s], 2), np.concatenate([-s, sign * c], 2)], axis=1)
        table = np.concatenate(split_table(table.reshape(512, -1)), axis=0)
        (odd if v % 2 else even).append(table)
    twiddle = np.stack([cosine[:32, :32], sine[:32, :32]])
    twiddle = np.tile(twiddle, (1, 1, PIX)).astype(np.float32)[:, :, None]
    twiddle = np.repeat(twiddle, ROWS, axis=2)
    u2 = np.arange(32)
    lanes = ((u2 % 4) * 32 + u2 // 4)[None, :] + 8 * np.arange(PIX)[:, None]
    small = np.zeros((2, 128, 128))
    for k in range(PIX):
        for e, table in enumerate((cosine, sine)):
            small[e, k * 32:(k + 1) * 32, lanes[k]] = table[:32, 0:N:32].T
    row = np.block([[small[0], -small[1]], [small[1], small[0]]]) / (N * 8.0)
    row = np.stack(split_table(row))
    return np.stack(even), np.stack(odd), row, twiddle


def swap_bit(first, second, width):
    clear = lax.broadcasted_iota(jnp.int32, first.shape, 1) % (2 * width) < width
    return (
        jnp.where(clear, first, pltpu.roll(second, width, 1)),
        jnp.where(clear, pltpu.roll(first, 128 - width, 1), second),
    )


def swap_bits(parts, widths):
    parts = list(parts)
    step = len(parts)
    for width in widths:
        step //= 2
        for n in range(len(parts)):
            if n // step % 2 == 0:
                parts[n], parts[n + step] = swap_bit(parts[n], parts[n + step], width)
    return parts


def sum_blocks(parts):
    lane = lax.broadcasted_iota(jnp.int32, parts[0].shape, 1)
    for width in (16, 8):
        clear = lane % (2 * width) < width
        half = len(parts) // 2
        sums = []
        for one, two in zip(parts[:half], parts[half:]):
            other = jnp.where(clear, two, one)
            other = jnp.where(
                clear, pltpu.roll(other, 128 - width, 1), pltpu.roll(other, width, 1))
            sums.append(jnp.where(clear, one, two) + other)
        parts = sums
    return parts[0]


def four_points(p):
    (ar, ai), (br, bi), (cr, ci), (dr, di) = p
    sr, si, er, ei = ar + cr, ai + ci, ar - cr, ai - ci
    tr, ti, fr, fi = br + dr, bi + di, br - dr, bi - di
    return [(sr + tr, si + ti), (er + fi, ei - fr), (sr - tr, si - ti), (er - fi, ei + fr)]


def eight_points(p):
    root = math.sqrt(0.5)
    even = four_points(p[0::2])
    odd = four_points(p[1::2])
    (r1, i1), (r2, i2), (r3, i3) = odd[1:]
    odd[1] = ((r1 + i1) * root, (i1 - r1) * root)
    odd[2] = (i2, -r2)
    odd[3] = ((i3 - r3) * root, -(r3 + i3) * root)
    out = [(e[0] + o[0], e[1] + o[1]) for e, o in zip(even, odd)]
    return out + [(e[0] - o[0], e[1] - o[1]) for e, o in zip(even, odd)]


def turn(p, step):
    if step == 0:
        return p
    c, s = math.cos(2.0 * math.pi * step / 32), math.sin(2.0 * math.pi * step / 32)
    return p[0] * c + p[1] * s, p[1] * c - p[0] * s


def split3(value):
    high = value.astype(BF16)
    rest = value - high.astype(F32)
    middle = rest.astype(BF16)
    return high, middle, (rest - middle.astype(F32)).astype(BF16)


def kernel(
    x_hbm, lab_hbm, phase_hbm, even_hbm, odd_hbm, row_hbm, twiddle_hbm, o_ref,
    x_v, lab_v, phase_v, even_v, odd_v, row_v, twiddle_v,
    xt, sbuf, rbuf, mixed, turned, lhs, cos_v, sin_v,
    wr, wi, psend, precv, zsend, zrecv, o_v,
    in_sem, send_sem, recv_sem, psend_sem, precv_sem, zsend_sem, zrecv_sem,
):
    me = lax.axis_index("scan")
    det = lax.axis_index("det")
    x, z = det // Z, det % Z

    x_copy = pltpu.make_async_copy(x_hbm, x_v, in_sem.at[0])
    lab_copies = [
        pltpu.make_async_copy(
            lab_hbm.at[:, :, pl.ds(m * 128, 128)], lab_v.at[m], in_sem.at[1])
        for m in range(8)
    ]
    phase_copies = [
        pltpu.make_async_copy(phase_hbm.at[:, pl.ds(m * 128, 128)], phase_v.at[m], in_sem.at[2])
        for m in range(8)
    ]
    row_copy = pltpu.make_async_copy(row_hbm, row_v, in_sem.at[3])
    twiddle_copy = pltpu.make_async_copy(twiddle_hbm, twiddle_v, in_sem.at[4])
    col_copies = [
        pltpu.make_async_copy(table.at[p % 2], to.at[p % 2], in_sem.at[6 + p])
        for p, (table, to) in enumerate([(even_hbm, even_v)] * 2 + [(odd_hbm, odd_v)] * 2)
    ]

    x_copy.start()
    col_copies[0].start()

    barrier = pltpu.get_barrier_semaphore()

    for i in range(1, SCAN):
        pl.semaphore_signal(
            barrier, inc=1, device_id=(lax.rem(me + i, SCAN), det), device_id_type=MESH)

    for i in range(1, 4):
        pl.semaphore_signal(
            barrier, inc=1, device_id=(me, lax.rem(x + i, X) * Z + z), device_id_type=MESH)
        pl.semaphore_signal(
            barrier, inc=1, device_id=(me, x * Z + lax.rem(z + i, Z)), device_id_type=MESH)

    for p in range(1, 4):
        col_copies[p].start()
    for copy in lab_copies + phase_copies:
        copy.start()
    row_copy.start()
    twiddle_copy.start()

    x_copy.wait()
    quarter = [[x_v[:, :, q * 256 + h * 128:q * 256 + (h + 1) * 128].reshape(128, 128)
                for q in range(4)] for h in range(2)]

    def put(value, at):
        value = jnp.transpose(value)
        high = value.astype(BF16)
        xt[at:at + 128, :128] = high
        xt[at:at + 128, 128:] = (value - high.astype(F32)).astype(BF16)

    for h, (x0, x1, x2, x3) in enumerate(quarter):
        put((x0 + x2) + (x1 + x3), h * 128)

    def column_part(p):
        col_copies[p].wait()
        table = even_v if p < 2 else odd_v
        rows = xt[p * 256:(p + 1) * 256] if p < 2 else xt[512:]
        prod = jnp.dot(table[p % 2], rows, preferred_element_type=F32)
        top = prod[:512] + prod[512:]
        sbuf[p] = (top[:, :128] + top[:, 128:]).reshape(SCAN, 2, ROWS, 128)

    column_part(0)
    for h, (x0, x1, x2, x3) in enumerate(quarter):
        put((x0 + x2) - (x1 + x3), 256 + h * 128)
    column_part(1)
    for h, (x0, x1, x2, x3) in enumerate(quarter):
        put(x0 - x2, 512 + h * 128)
        put(x1 - x3, 768 + h * 128)
    column_part(2)
    column_part(3)

    pl.semaphore_wait(barrier, SCAN - 1 + X - 1 + Z - 1)
    chip = lax.div(me, 2)

    def send_part(p):
        @pl.loop(0, 32)
        def _(i):
            to = lax.rem(chip + 1 + lax.rem(i, 16), 16) * 2 + lax.div(i, 16)

            @pl.when(to != me)
            def _():
                pltpu.make_async_remote_copy(
                    src_ref=sbuf.at[p, to],
                    dst_ref=rbuf.at[p, me],
                    send_sem=send_sem.at[p],
                    recv_sem=recv_sem.at[p],
                    device_id=(to, det),
                    device_id_type=MESH,
                ).start()

    def wait_sent(p):
        most = rbuf.at[p, pl.ds(0, SCAN - 1)]
        pltpu.make_async_copy(most, most, send_sem.at[p]).wait()

    send_part(0)
    send_part(1)
    for p in range(4):
        rbuf[p, me] = sbuf[p, me]

    pltpu.make_async_copy(phase_v, phase_v, in_sem.at[2]).wait()
    cos_v[...] = jnp.cos(phase_v[...])
    sin_v[...] = jnp.sin(phase_v[...])
    pltpu.make_async_copy(lab_v, lab_v, in_sem.at[1]).wait()
    for p, v in enumerate(PARTS):
        reals, imags = [], []
        for k in range(PIX):
            for m in range(8):
                cosine = cos_v[m, pl.ds(v, ROWS, stride=4), :]
                sine = sin_v[m, pl.ds(v, ROWS, stride=4), :]
                zero = jnp.zeros_like(cosine)
                labels = lab_v[m, k, pl.ds(v, ROWS, stride=4), :]
                left = labels == 1
                right = labels == 2
                reals.append(jnp.where(left, cosine, jnp.where(right, -cosine, zero)))
                imags.append(jnp.where(jnp.logical_or(left, right), -sine, zero))
        for to, parts in ((wr, reals), (wi, imags)):
            for u1, part in enumerate(swap_bits(parts, (16, 8, 4, 2, 1))):
                to[p, u1] = part

    row_copy.wait()
    twiddle_copy.wait()

    def row_part(p):
        most = rbuf.at[p, pl.ds(0, SCAN - 1)]
        pltpu.make_async_copy(most, most, recv_sem.at[p]).wait()
        for e in range(4):
            points = [(rbuf[p, 4 * g + e, 0], rbuf[p, 4 * g + e, 1]) for g in range(8)]
            for b, point in enumerate(eight_points(points)):
                mixed[e, b, 0], mixed[e, b, 1] = turn(point, e * b)
        for b in range(8):
            points = four_points([(mixed[e, b, 0], mixed[e, b, 1]) for e in range(4)])
            for c, (re, im) in enumerate(points):
                u1 = b + 8 * c
                cosine, sine = twiddle_v[0, u1], twiddle_v[1, u1]
                turned[u1 * ROWS:(u1 + 1) * ROWS, :128] = re * cosine + im * sine
                turned[u1 * ROWS:(u1 + 1) * ROWS, 128:] = im * cosine - re * sine
        for qh in range(2):
            value = turned[qh * 128:(qh + 1) * 128]
            high = value.astype(BF16)
            lhs[qh, :128] = high
            lhs[qh, 128:] = (value - high.astype(F32)).astype(BF16)
            both = jnp.dot(lhs[qh], row_v[0], preferred_element_type=F32)
            low = jnp.dot(lhs[qh, :128], row_v[1], preferred_element_type=F32)
            spec = both[:128] + both[128:] + low
            sums = [], []
            for ql in range(4):
                reals, imags = [], []
                for e in range(4):
                    at = ql * 4 + e
                    re = spec[at * ROWS:(at + 1) * ROWS, :128]
                    im = spec[at * ROWS:(at + 1) * ROWS, 128:]
                    w_re, w_im = wr[p, qh * 16 + at], wi[p, qh * 16 + at]
                    reals.append(re * w_re - im * w_im)
                    imags.append(re * w_im + im * w_re)
                sums[0].append(sum_blocks(reals))
                sums[1].append(sum_blocks(imags))
            for e in range(2):
                for q, part in enumerate(swap_bits(sums[e], (4, 2))):
                    psend[p, q, qh, e] = part

        @pl.loop(1, X)
        def _(j):
            q = (x + j) % X
            pltpu.make_async_remote_copy(
                src_ref=psend.at[p, q],
                dst_ref=precv.at[p, j - 1],
                send_sem=psend_sem.at[p],
                recv_sem=precv_sem.at[p],
                device_id=(me, q * Z + z),
                device_id_type=MESH,
            ).start()

    def sum_x(p):
        pltpu.make_async_copy(precv.at[p], precv.at[p], precv_sem.at[p]).wait()
        parts = []
        for qh in range(2):
            for e in range(2):
                total = psend[p, x, qh, e]
                for j in range(X - 1):
                    total = total + precv[p, j, qh, e]
                parts.append(total)
        for h, part in enumerate(swap_bits(parts, (1, 64))):
            zsend[p, h] = part

        @pl.loop(1, Z)
        def _(j):
            to = (z + j) % Z
            pltpu.make_async_remote_copy(
                src_ref=zsend.at[p, to],
                dst_ref=zrecv.at[p, j - 1],
                send_sem=zsend_sem.at[p],
                recv_sem=zrecv_sem.at[p],
                device_id=(me, x * Z + to),
                device_id_type=MESH,
            ).start()

    @pl.loop(0, 4)
    def _(p):
        @pl.when(p < 2)
        def _():
            wait_sent(p)
            send_part(p + 2)

        @pl.when(p > 0)
        def _():
            sum_x(p - 1)

        row_part(p)

    sum_x(3)

    lane = lax.broadcasted_iota(jnp.int32, (128, 128), 0)
    target = (
        lane // 32 * 32 + (lane % 2 * 4 + lane // 2 % 4) * 4 + lane // 8 % 4)
    order = jnp.where(
        target == lax.broadcasted_iota(jnp.int32, (128, 128), 1), 1.0, 0.0).astype(BF16)
    results = []
    for p in range(4):
        pltpu.make_async_copy(zrecv.at[p], zrecv.at[p], zrecv_sem.at[p]).wait()
        results.append(zsend[p, z] + zrecv[p, 0] + zrecv[p, 1] + zrecv[p, 2])
    result = jnp.concatenate(results, axis=0)
    moved = jnp.dot(jnp.concatenate(split3(result), axis=0), order, preferred_element_type=F32)
    result = moved[:BLOCK] + moved[BLOCK:2 * BLOCK] + moved[2 * BLOCK:]
    other = pltpu.roll(result, 64, 1)
    for p, v in enumerate(PARTS):
        o_v[0, pl.ds(v, ROWS, stride=4), :] = result[p * ROWS:(p + 1) * ROWS]
        o_v[1, pl.ds(v, ROWS, stride=4), :] = other[p * ROWS:(p + 1) * ROWS]
    o_ref[...] = o_v[:, :, :N // (X * Z)]

    for p in range(4):
        if p >= 2:
            wait_sent(p)
        pltpu.make_async_copy(precv.at[p], precv.at[p], psend_sem.at[p]).wait()
        pltpu.make_async_copy(zrecv.at[p], zrecv.at[p], zsend_sem.at[p]).wait()


def local(even, odd, row, twiddle, intensities, trotter_labels, phase_shift):
    any_spec = pl.BlockSpec(memory_space=pl.ANY)
    dma = pltpu.SemaphoreType.DMA
    return pl.pallas_call(
        kernel,
        out_shape=jax.ShapeDtypeStruct((2, BLOCK, N // (X * Z)), F32),
        in_specs=[any_spec] * 7,
        out_specs=pl.BlockSpec(memory_space=pltpu.VMEM),
        scratch_shapes=[
            pltpu.VMEM((PIX, BLOCK, N), F32),
            pltpu.VMEM((8, PIX, BLOCK, 128), jnp.int32),
            pltpu.VMEM((8, BLOCK, 128), F32),
            pltpu.VMEM((2, 1024, 256), BF16),
            pltpu.VMEM((2, 1024, 512), BF16),
            pltpu.VMEM((2, 256, 256), BF16),
            pltpu.VMEM((2, 32, ROWS, 128), F32),
            pltpu.VMEM((N, 256), BF16),
            pltpu.VMEM((4, SCAN, 2, ROWS, 128), F32),
            pltpu.VMEM((4, SCAN, 2, ROWS, 128), F32),
            pltpu.VMEM((4, 8, 2, ROWS, 128), F32),
            pltpu.VMEM((256, 256), F32),
            pltpu.VMEM((2, 256, 256), BF16),
            pltpu.VMEM((8, BLOCK, 128), F32),
            pltpu.VMEM((8, BLOCK, 128), F32),
            pltpu.VMEM((4, 32, ROWS, 128), F32),
            pltpu.VMEM((4, 32, ROWS, 128), F32),
            pltpu.VMEM((4, X, 2, 2, ROWS, 128), F32),
            pltpu.VMEM((4, X - 1, 2, 2, ROWS, 128), F32),
            pltpu.VMEM((4, Z, ROWS, 128), F32),
            pltpu.VMEM((4, Z - 1, ROWS, 128), F32),
            pltpu.VMEM((2, BLOCK, 128), F32),
            dma((10,)),
            dma((4,)),
            dma((4,)),
            dma((4,)),
            dma((4,)),
            dma((4,)),
            dma((4,)),
        ],
        compiler_params=pltpu.CompilerParams(
            collective_id=0, has_side_effects=True, vmem_limit_bytes=55140 * 1024),
        name="ptycho",
    )(intensities, trotter_labels, phase_shift, even, odd, row, twiddle)


def solution(mesh):
    tables = make_tables()
    placed = (P("det", "scan", None), P("det", "scan", None), P("scan", None))
    fixed = tuple(P(*[None] * table.ndim) for table in tables)
    mapped = jax.shard_map(
        local, mesh=mesh, in_specs=fixed + placed, out_specs=P(None, "scan", "det"),
        check_vma=False)

    def run(intensities, trotter_labels, phase_shift):
        return mapped(*map(jnp.asarray, tables), intensities, trotter_labels, phase_shift)

    return run
```

```python
import math

import jax
import jax.numpy as jnp
import ml_dtypes
import numpy as np
from jax import lax
from jax.experimental import pallas as pl
from jax.experimental.pallas import tpu as pltpu
from jax.sharding import PartitionSpec as P

MESH = pl.DeviceIdType.MESH
F32 = jnp.float32
BF16 = jnp.bfloat16

N = 1024
SCAN = 32
BLOCK = 32
PARTS = (0, 2, 1, 3)
ROWS = BLOCK // 4
PIX = 4
X = 4
Z = 4


def split_table(table):
    high = table.astype(ml_dtypes.bfloat16)
    low = (table - high.astype(np.float64)).astype(ml_dtypes.bfloat16)
    return high, low


def make_tables():
    index = np.arange(N)
    angles = (index[:, None] * index[None, :] % N) * (2.0 * math.pi / N)
    cosine, sine = np.cos(angles), np.sin(angles)
    cos_v = cosine[:, :256].reshape(SCAN, ROWS, 4, 256)
    sin_v = sine[:, :256].reshape(SCAN, ROWS, 4, 256)
    even, odd = [], []
    for v in PARTS:
        c, s = cos_v[:, :, v], sin_v[:, :, v]
        if v % 2 == 0:
            table = np.stack([c, -s], axis=1)
        else:
            sign = 1.0 if v == 3 else -1.0
            table = np.stack(
                [np.concatenate([c, sign * s], 2), np.concatenate([-s, sign * c], 2)], axis=1)
        table = np.concatenate(split_table(table.reshape(512, -1)), axis=0)
        (odd if v % 2 else even).append(table)
    twiddle = np.stack([cosine[:32, :32], sine[:32, :32]])
    twiddle = np.tile(twiddle, (1, 1, PIX)).astype(np.float32)[:, :, None]
    twiddle = np.repeat(twiddle, ROWS, axis=2)
    u2 = np.arange(32)
    lanes = ((u2 % 4) * 32 + u2 // 4)[None, :] + 8 * np.arange(PIX)[:, None]
    small = np.zeros((2, 128, 128))
    for k in range(PIX):
        for e, table in enumerate((cosine, sine)):
            small[e, k * 32:(k + 1) * 32, lanes[k]] = table[:32, 0:N:32].T
    row = np.block([[small[0], -small[1]], [small[1], small[0]]]) / (N * 8.0)
    row = np.stack(split_table(row))
    return np.stack(even), np.stack(odd), row, twiddle


def swap_bit(first, second, width):
    clear = lax.broadcasted_iota(jnp.int32, first.shape, 1) % (2 * width) < width
    return (
        jnp.where(clear, first, pltpu.roll(second, width, 1)),
        jnp.where(clear, pltpu.roll(first, 128 - width, 1), second),
    )


def swap_bits(parts, widths):
    parts = list(parts)
    step = len(parts)
    for width in widths:
        step //= 2
        for n in range(len(parts)):
            if n // step % 2 == 0:
                parts[n], parts[n + step] = swap_bit(parts[n], parts[n + step], width)
    return parts


def sum_blocks(parts):
    lane = lax.broadcasted_iota(jnp.int32, parts[0].shape, 1)
    for width in (16, 8):
        clear = lane % (2 * width) < width
        half = len(parts) // 2
        sums = []
        for one, two in zip(parts[:half], parts[half:]):
            other = jnp.where(clear, two, one)
            other = jnp.where(
                clear, pltpu.roll(other, 128 - width, 1), pltpu.roll(other, width, 1))
            sums.append(jnp.where(clear, one, two) + other)
        parts = sums
    return parts[0]


def four_points(p):
    (ar, ai), (br, bi), (cr, ci), (dr, di) = p
    sr, si, er, ei = ar + cr, ai + ci, ar - cr, ai - ci
    tr, ti, fr, fi = br + dr, bi + di, br - dr, bi - di
    return [(sr + tr, si + ti), (er + fi, ei - fr), (sr - tr, si - ti), (er - fi, ei + fr)]


def eight_points(p):
    root = math.sqrt(0.5)
    even = four_points(p[0::2])
    odd = four_points(p[1::2])
    (r1, i1), (r2, i2), (r3, i3) = odd[1:]
    odd[1] = ((r1 + i1) * root, (i1 - r1) * root)
    odd[2] = (i2, -r2)
    odd[3] = ((i3 - r3) * root, -(r3 + i3) * root)
    out = [(e[0] + o[0], e[1] + o[1]) for e, o in zip(even, odd)]
    return out + [(e[0] - o[0], e[1] - o[1]) for e, o in zip(even, odd)]


def turn(p, step):
    if step == 0:
        return p
    c, s = math.cos(2.0 * math.pi * step / 32), math.sin(2.0 * math.pi * step / 32)
    return p[0] * c + p[1] * s, p[1] * c - p[0] * s


def split3(value):
    high = value.astype(BF16)
    rest = value - high.astype(F32)
    middle = rest.astype(BF16)
    return high, middle, (rest - middle.astype(F32)).astype(BF16)


def kernel(
    x_hbm, lab_hbm, phase_hbm, even_hbm, odd_hbm, row_hbm, twiddle_hbm, o_ref,
    x_v, lab_v, phase_v, even_v, odd_v, row_v, twiddle_v,
    xt, sbuf, rbuf, mixed, turned, lhs, cos_v, sin_v,
    wr, wi, psend, precv, zsend, zrecv, o_v,
    in_sem, send_sem, recv_sem, psend_sem, precv_sem, zsend_sem, zrecv_sem,
):
    me = lax.axis_index("scan")
    det = lax.axis_index("det")
    x, z = det // Z, det % Z

    x_copy = pltpu.make_async_copy(x_hbm, x_v, in_sem.at[0])
    lab_copies = [
        pltpu.make_async_copy(
            lab_hbm.at[:, :, pl.ds(m * 128, 128)], lab_v.at[m], in_sem.at[1])
        for m in range(8)
    ]
    phase_copies = [
        pltpu.make_async_copy(phase_hbm.at[:, pl.ds(m * 128, 128)], phase_v.at[m], in_sem.at[2])
        for m in range(8)
    ]
    row_copy = pltpu.make_async_copy(row_hbm, row_v, in_sem.at[3])
    twiddle_copy = pltpu.make_async_copy(twiddle_hbm, twiddle_v, in_sem.at[4])
    col_copies = [
        pltpu.make_async_copy(table.at[p % 2], to.at[p % 2], in_sem.at[6 + p])
        for p, (table, to) in enumerate([(even_hbm, even_v)] * 2 + [(odd_hbm, odd_v)] * 2)
    ]

    x_copy.start()
    col_copies[0].start()

    barrier = pltpu.get_barrier_semaphore()

    for i in range(1, SCAN):
        pl.semaphore_signal(
            barrier, inc=1, device_id=(lax.rem(me + i, SCAN), det), device_id_type=MESH)

    for i in range(1, 4):
        pl.semaphore_signal(
            barrier, inc=1, device_id=(me, lax.rem(x + i, X) * Z + z), device_id_type=MESH)
        pl.semaphore_signal(
            barrier, inc=1, device_id=(me, x * Z + lax.rem(z + i, Z)), device_id_type=MESH)

    for p in range(1, 4):
        col_copies[p].start()
    for copy in lab_copies + phase_copies:
        copy.start()
    row_copy.start()
    twiddle_copy.start()

    x_copy.wait()
    quarter = [[x_v[:, :, q * 256 + h * 128:q * 256 + (h + 1) * 128].reshape(128, 128)
                for q in range(4)] for h in range(2)]

    def put(value, at):
        value = jnp.transpose(value)
        high = value.astype(BF16)
        xt[at:at + 128, :128] = high
        xt[at:at + 128, 128:] = (value - high.astype(F32)).astype(BF16)

    for h, (x0, x1, x2, x3) in enumerate(quarter):
        put((x0 + x2) + (x1 + x3), h * 128)

    def column_part(p):
        col_copies[p].wait()
        table = even_v if p < 2 else odd_v
        rows = xt[p * 256:(p + 1) * 256] if p < 2 else xt[512:]
        prod = jnp.dot(table[p % 2], rows, preferred_element_type=F32)
        top = prod[:512] + prod[512:]
        sbuf[p] = (top[:, :128] + top[:, 128:]).reshape(SCAN, 2, ROWS, 128)

    chip = lax.div(me, 2)

    def send_part(p):
        @pl.loop(0, 32)
        def _(i):
            to = lax.rem(chip + 1 + lax.rem(i, 16), 16) * 2 + lax.div(i, 16)

            @pl.when(to != me)
            def _():
                pltpu.make_async_remote_copy(
                    src_ref=sbuf.at[p, to],
                    dst_ref=rbuf.at[p, me],
                    send_sem=send_sem.at[p],
                    recv_sem=recv_sem.at[p],
                    device_id=(to, det),
                    device_id_type=MESH,
                ).start()

    def wait_sent(p):
        most = rbuf.at[p, pl.ds(0, SCAN - 1)]
        pltpu.make_async_copy(most, most, send_sem.at[p]).wait()

    column_part(0)
    pl.semaphore_wait(barrier, SCAN - 1 + X - 1 + Z - 1)
    send_part(0)
    for h, (x0, x1, x2, x3) in enumerate(quarter):
        put((x0 + x2) - (x1 + x3), 256 + h * 128)
    column_part(1)
    send_part(1)
    for h, (x0, x1, x2, x3) in enumerate(quarter):
        put(x0 - x2, 512 + h * 128)
        put(x1 - x3, 768 + h * 128)
    column_part(2)
    column_part(3)
    for p in range(4):
        rbuf[p, me] = sbuf[p, me]

    pltpu.make_async_copy(phase_v, phase_v, in_sem.at[2]).wait()
    cos_v[...] = jnp.cos(phase_v[...])
    sin_v[...] = jnp.sin(phase_v[...])
    pltpu.make_async_copy(lab_v, lab_v, in_sem.at[1]).wait()
    for p, v in enumerate(PARTS):
        reals, imags = [], []
        for k in range(PIX):
            for m in range(8):
                cosine = cos_v[m, pl.ds(v, ROWS, stride=4), :]
                sine = sin_v[m, pl.ds(v, ROWS, stride=4), :]
                zero = jnp.zeros_like(cosine)
                labels = lab_v[m, k, pl.ds(v, ROWS, stride=4), :]
                left = labels == 1
                right = labels == 2
                reals.append(jnp.where(left, cosine, jnp.where(right, -cosine, zero)))
                imags.append(jnp.where(jnp.logical_or(left, right), -sine, zero))
        for to, parts in ((wr, reals), (wi, imags)):
            for u1, part in enumerate(swap_bits(parts, (16, 8, 4, 2, 1))):
                to[p, u1] = part

    row_copy.wait()
    twiddle_copy.wait()

    def row_part(p):
        most = rbuf.at[p, pl.ds(0, SCAN - 1)]
        pltpu.make_async_copy(most, most, recv_sem.at[p]).wait()
        for e in range(4):
            points = [(rbuf[p, 4 * g + e, 0], rbuf[p, 4 * g + e, 1]) for g in range(8)]
            for b, point in enumerate(eight_points(points)):
                mixed[e, b, 0], mixed[e, b, 1] = turn(point, e * b)
        for b in range(8):
            points = four_points([(mixed[e, b, 0], mixed[e, b, 1]) for e in range(4)])
            for c, (re, im) in enumerate(points):
                u1 = b + 8 * c
                cosine, sine = twiddle_v[0, u1], twiddle_v[1, u1]
                turned[u1 * ROWS:(u1 + 1) * ROWS, :128] = re * cosine + im * sine
                turned[u1 * ROWS:(u1 + 1) * ROWS, 128:] = im * cosine - re * sine
        for qh in range(2):
            value = turned[qh * 128:(qh + 1) * 128]
            high = value.astype(BF16)
            lhs[qh, :128] = high
            lhs[qh, 128:] = (value - high.astype(F32)).astype(BF16)
            both = jnp.dot(lhs[qh], row_v[0], preferred_element_type=F32)
            low = jnp.dot(lhs[qh, :128], row_v[1], preferred_element_type=F32)
            spec = both[:128] + both[128:] + low
            sums = [], []
            for ql in range(4):
                reals, imags = [], []
                for e in range(4):
                    at = ql * 4 + e
                    re = spec[at * ROWS:(at + 1) * ROWS, :128]
                    im = spec[at * ROWS:(at + 1) * ROWS, 128:]
                    w_re, w_im = wr[p, qh * 16 + at], wi[p, qh * 16 + at]
                    reals.append(re * w_re - im * w_im)
                    imags.append(re * w_im + im * w_re)
                sums[0].append(sum_blocks(reals))
                sums[1].append(sum_blocks(imags))
            for e in range(2):
                for q, part in enumerate(swap_bits(sums[e], (4, 2))):
                    psend[p, q, qh, e] = part

        @pl.loop(1, X)
        def _(j):
            q = (x + j) % X
            pltpu.make_async_remote_copy(
                src_ref=psend.at[p, q],
                dst_ref=precv.at[p, j - 1],
                send_sem=psend_sem.at[p],
                recv_sem=precv_sem.at[p],
                device_id=(me, q * Z + z),
                device_id_type=MESH,
            ).start()

    def sum_x(p):
        pltpu.make_async_copy(precv.at[p], precv.at[p], precv_sem.at[p]).wait()
        parts = []
        for qh in range(2):
            for e in range(2):
                total = psend[p, x, qh, e]
                for j in range(X - 1):
                    total = total + precv[p, j, qh, e]
                parts.append(total)
        for h, part in enumerate(swap_bits(parts, (1, 64))):
            zsend[p, h] = part

        @pl.loop(1, Z)
        def _(j):
            to = (z + j) % Z
            pltpu.make_async_remote_copy(
                src_ref=zsend.at[p, to],
                dst_ref=zrecv.at[p, j - 1],
                send_sem=zsend_sem.at[p],
                recv_sem=zrecv_sem.at[p],
                device_id=(me, x * Z + to),
                device_id_type=MESH,
            ).start()

    @pl.loop(0, 4)
    def _(p):
        @pl.when(p < 2)
        def _():
            wait_sent(p)
            send_part(p + 2)

        @pl.when(p > 0)
        def _():
            sum_x(p - 1)

        row_part(p)

    sum_x(3)

    lane = lax.broadcasted_iota(jnp.int32, (128, 128), 0)
    target = (
        lane // 32 * 32 + (lane % 2 * 4 + lane // 2 % 4) * 4 + lane // 8 % 4)
    order = jnp.where(
        target == lax.broadcasted_iota(jnp.int32, (128, 128), 1), 1.0, 0.0).astype(BF16)
    results = []
    for p in range(4):
        pltpu.make_async_copy(zrecv.at[p], zrecv.at[p], zrecv_sem.at[p]).wait()
        results.append(zsend[p, z] + zrecv[p, 0] + zrecv[p, 1] + zrecv[p, 2])
    result = jnp.concatenate(results, axis=0)
    moved = jnp.dot(jnp.concatenate(split3(result), axis=0), order, preferred_element_type=F32)
    result = moved[:BLOCK] + moved[BLOCK:2 * BLOCK] + moved[2 * BLOCK:]
    other = pltpu.roll(result, 64, 1)
    for p, v in enumerate(PARTS):
        o_v[0, pl.ds(v, ROWS, stride=4), :] = result[p * ROWS:(p + 1) * ROWS]
        o_v[1, pl.ds(v, ROWS, stride=4), :] = other[p * ROWS:(p + 1) * ROWS]
    o_ref[...] = o_v[:, :, :N // (X * Z)]

    for p in range(4):
        if p >= 2:
            wait_sent(p)
        pltpu.make_async_copy(precv.at[p], precv.at[p], psend_sem.at[p]).wait()
        pltpu.make_async_copy(zrecv.at[p], zrecv.at[p], zsend_sem.at[p]).wait()


def local(even, odd, row, twiddle, intensities, trotter_labels, phase_shift):
    any_spec = pl.BlockSpec(memory_space=pl.ANY)
    dma = pltpu.SemaphoreType.DMA
    return pl.pallas_call(
        kernel,
        out_shape=jax.ShapeDtypeStruct((2, BLOCK, N // (X * Z)), F32),
        in_specs=[any_spec] * 7,
        out_specs=pl.BlockSpec(memory_space=pltpu.VMEM),
        scratch_shapes=[
            pltpu.VMEM((PIX, BLOCK, N), F32),
            pltpu.VMEM((8, PIX, BLOCK, 128), jnp.int32),
            pltpu.VMEM((8, BLOCK, 128), F32),
            pltpu.VMEM((2, 1024, 256), BF16),
            pltpu.VMEM((2, 1024, 512), BF16),
            pltpu.VMEM((2, 256, 256), BF16),
            pltpu.VMEM((2, 32, ROWS, 128), F32),
            pltpu.VMEM((N, 256), BF16),
            pltpu.VMEM((4, SCAN, 2, ROWS, 128), F32),
            pltpu.VMEM((4, SCAN, 2, ROWS, 128), F32),
            pltpu.VMEM((4, 8, 2, ROWS, 128), F32),
            pltpu.VMEM((256, 256), F32),
            pltpu.VMEM((2, 256, 256), BF16),
            pltpu.VMEM((8, BLOCK, 128), F32),
            pltpu.VMEM((8, BLOCK, 128), F32),
            pltpu.VMEM((4, 32, ROWS, 128), F32),
            pltpu.VMEM((4, 32, ROWS, 128), F32),
            pltpu.VMEM((4, X, 2, 2, ROWS, 128), F32),
            pltpu.VMEM((4, X - 1, 2, 2, ROWS, 128), F32),
            pltpu.VMEM((4, Z, ROWS, 128), F32),
            pltpu.VMEM((4, Z - 1, ROWS, 128), F32),
            pltpu.VMEM((2, BLOCK, 128), F32),
            dma((10,)),
            dma((4,)),
            dma((4,)),
            dma((4,)),
            dma((4,)),
            dma((4,)),
            dma((4,)),
        ],
        compiler_params=pltpu.CompilerParams(
            collective_id=0, has_side_effects=True, vmem_limit_bytes=55140 * 1024),
        name="ptycho",
    )(intensities, trotter_labels, phase_shift, even, odd, row, twiddle)


def solution(mesh):
    tables = make_tables()
    placed = (P("det", "scan", None), P("det", "scan", None), P("scan", None))
    fixed = tuple(P(*[None] * table.ndim) for table in tables)
    mapped = jax.shard_map(
        local, mesh=mesh, in_specs=fixed + placed, out_specs=P(None, "scan", "det"),
        check_vma=False)

    def run(intensities, trotter_labels, phase_shift):
        return mapped(*map(jnp.asarray, tables), intensities, trotter_labels, phase_shift)

    return run
```

```python
import math

import jax
import jax.numpy as jnp
import ml_dtypes
import numpy as np
from jax import lax
from jax.experimental import pallas as pl
from jax.experimental.pallas import tpu as pltpu
from jax.sharding import PartitionSpec as P

MESH = pl.DeviceIdType.MESH
F32 = jnp.float32
BF16 = jnp.bfloat16

N = 1024
SCAN = 32
BLOCK = 32
PARTS = (0, 2, 1, 3)
ROWS = BLOCK // 4
PIX = 4
X = 4
Z = 4


def split_table(table):
    high = table.astype(ml_dtypes.bfloat16)
    low = (table - high.astype(np.float64)).astype(ml_dtypes.bfloat16)
    return high, low


def make_tables():
    index = np.arange(N)
    angles = (index[:, None] * index[None, :] % N) * (2.0 * math.pi / N)
    cosine, sine = np.cos(angles), np.sin(angles)
    cos_v = cosine[:, :256].reshape(SCAN, ROWS, 4, 256)
    sin_v = sine[:, :256].reshape(SCAN, ROWS, 4, 256)
    even, odd = [], []
    for v in PARTS:
        c, s = cos_v[:, :, v], sin_v[:, :, v]
        if v % 2 == 0:
            table = np.stack([c, -s], axis=1)
        else:
            sign = 1.0 if v == 3 else -1.0
            table = np.stack(
                [np.concatenate([c, sign * s], 2), np.concatenate([-s, sign * c], 2)], axis=1)
        table = np.concatenate(split_table(table.reshape(512, -1)), axis=0)
        (odd if v % 2 else even).append(table)
    twiddle = np.stack([cosine[:32, :32], sine[:32, :32]])
    twiddle = np.tile(twiddle, (1, 1, PIX)).astype(np.float32)[:, :, None]
    twiddle = np.repeat(twiddle, ROWS, axis=2)
    u2 = np.arange(32)
    lanes = ((u2 % 4) * 32 + u2 // 4)[None, :] + 8 * np.arange(PIX)[:, None]
    small = np.zeros((2, 128, 128))
    for k in range(PIX):
        for e, table in enumerate((cosine, sine)):
            small[e, k * 32:(k + 1) * 32, lanes[k]] = table[:32, 0:N:32].T
    row = np.block([[small[0], -small[1]], [small[1], small[0]]]) / (N * 8.0)
    row = np.stack(split_table(row))
    return np.stack(even), np.stack(odd), row, twiddle


def swap_bit(first, second, width):
    clear = lax.broadcasted_iota(jnp.int32, first.shape, 1) % (2 * width) < width
    return (
        jnp.where(clear, first, pltpu.roll(second, width, 1)),
        jnp.where(clear, pltpu.roll(first, 128 - width, 1), second),
    )


def swap_bits(parts, widths):
    parts = list(parts)
    step = len(parts)
    for width in widths:
        step //= 2
        for n in range(len(parts)):
            if n // step % 2 == 0:
                parts[n], parts[n + step] = swap_bit(parts[n], parts[n + step], width)
    return parts


def sum_blocks(parts):
    lane = lax.broadcasted_iota(jnp.int32, parts[0].shape, 1)
    for width in (16, 8):
        clear = lane % (2 * width) < width
        half = len(parts) // 2
        sums = []
        for one, two in zip(parts[:half], parts[half:]):
            other = jnp.where(clear, two, one)
            other = jnp.where(
                clear, pltpu.roll(other, 128 - width, 1), pltpu.roll(other, width, 1))
            sums.append(jnp.where(clear, one, two) + other)
        parts = sums
    return parts[0]


def four_points(p):
    (ar, ai), (br, bi), (cr, ci), (dr, di) = p
    sr, si, er, ei = ar + cr, ai + ci, ar - cr, ai - ci
    tr, ti, fr, fi = br + dr, bi + di, br - dr, bi - di
    return [(sr + tr, si + ti), (er + fi, ei - fr), (sr - tr, si - ti), (er - fi, ei + fr)]


def eight_points(p):
    root = math.sqrt(0.5)
    even = four_points(p[0::2])
    odd = four_points(p[1::2])
    (r1, i1), (r2, i2), (r3, i3) = odd[1:]
    odd[1] = ((r1 + i1) * root, (i1 - r1) * root)
    odd[2] = (i2, -r2)
    odd[3] = ((i3 - r3) * root, -(r3 + i3) * root)
    out = [(e[0] + o[0], e[1] + o[1]) for e, o in zip(even, odd)]
    return out + [(e[0] - o[0], e[1] - o[1]) for e, o in zip(even, odd)]


def turn(p, step):
    if step == 0:
        return p
    c, s = math.cos(2.0 * math.pi * step / 32), math.sin(2.0 * math.pi * step / 32)
    return p[0] * c + p[1] * s, p[1] * c - p[0] * s


def split3(value):
    high = value.astype(BF16)
    rest = value - high.astype(F32)
    middle = rest.astype(BF16)
    return high, middle, (rest - middle.astype(F32)).astype(BF16)


def kernel(
    x_hbm, lab_hbm, phase_hbm, even_hbm, odd_hbm, row_hbm, twiddle_hbm, o_ref,
    x_v, lab_v, phase_v, even_v, odd_v, row_v, twiddle_v,
    xt, sbuf, rbuf, mixed, turned, lhs, cos_v, sin_v,
    wr, wi, psend, precv, zsend, zrecv, o_v,
    in_sem, send_sem, recv_sem, psend_sem, precv_sem, zsend_sem, zrecv_sem,
):
    me = lax.axis_index("scan")
    det = lax.axis_index("det")
    x, z = det // Z, det % Z

    x_copy = pltpu.make_async_copy(x_hbm, x_v, in_sem.at[0])
    lab_copies = [
        pltpu.make_async_copy(
            lab_hbm.at[:, :, pl.ds(m * 128, 128)], lab_v.at[m], in_sem.at[1])
        for m in range(8)
    ]
    phase_copies = [
        pltpu.make_async_copy(phase_hbm.at[:, pl.ds(m * 128, 128)], phase_v.at[m], in_sem.at[2])
        for m in range(8)
    ]
    row_copy = pltpu.make_async_copy(row_hbm, row_v, in_sem.at[3])
    twiddle_copy = pltpu.make_async_copy(twiddle_hbm, twiddle_v, in_sem.at[4])
    col_copies = [
        pltpu.make_async_copy(table.at[p % 2], to.at[p % 2], in_sem.at[6 + p])
        for p, (table, to) in enumerate([(even_hbm, even_v)] * 2 + [(odd_hbm, odd_v)] * 2)
    ]

    x_copy.start()
    col_copies[0].start()

    barrier = pltpu.get_barrier_semaphore()

    for i in range(1, SCAN):
        pl.semaphore_signal(
            barrier, inc=1, device_id=(lax.rem(me + i, SCAN), det), device_id_type=MESH)

    for i in range(1, 4):
        pl.semaphore_signal(
            barrier, inc=1, device_id=(me, lax.rem(x + i, X) * Z + z), device_id_type=MESH)
        pl.semaphore_signal(
            barrier, inc=1, device_id=(me, x * Z + lax.rem(z + i, Z)), device_id_type=MESH)

    for p in range(1, 4):
        col_copies[p].start()
    for copy in lab_copies + phase_copies:
        copy.start()
    row_copy.start()
    twiddle_copy.start()

    x_copy.wait()
    quarter = [[x_v[:, :, q * 256 + h * 128:q * 256 + (h + 1) * 128].reshape(128, 128)
                for q in range(4)] for h in range(2)]

    def put(value, at):
        value = jnp.transpose(value)
        high = value.astype(BF16)
        xt[at:at + 128, :128] = high
        xt[at:at + 128, 128:] = (value - high.astype(F32)).astype(BF16)

    for h, (x0, x1, x2, x3) in enumerate(quarter):
        put((x0 + x2) + (x1 + x3), h * 128)

    def column_part(p):
        col_copies[p].wait()
        table = even_v if p < 2 else odd_v
        rows = xt[p * 256:(p + 1) * 256] if p < 2 else xt[512:]
        prod = jnp.dot(table[p % 2], rows, preferred_element_type=F32)
        top = prod[:512] + prod[512:]
        sbuf[p] = (top[:, :128] + top[:, 128:]).reshape(SCAN, 2, ROWS, 128)

    chip, own = lax.div(me, 2), lax.rem(me, 2)

    def send_chunk(q):
        p, core = lax.div(q, 2), lax.rem(q, 2)

        @pl.loop(1, 17)
        def _(i):
            to = lax.rem(chip + i, 16) * 2 + core

            @pl.when(to != me)
            def _():
                pltpu.make_async_remote_copy(
                    src_ref=sbuf.at[p, to],
                    dst_ref=rbuf.at[p, me],
                    send_sem=send_sem.at[q],
                    recv_sem=recv_sem.at[p],
                    device_id=(to, det),
                    device_id_type=MESH,
                ).start()

    def wait_sent(q):
        same = lax.rem(q, 2) == own
        for mine, count in ((same, 15), (jnp.logical_not(same), 16)):
            @pl.when(mine)
            def _(count=count):
                most = rbuf.at[0, pl.ds(0, count)]
                pltpu.make_async_copy(most, most, send_sem.at[q]).wait()

    column_part(0)
    pl.semaphore_wait(barrier, SCAN - 1 + X - 1 + Z - 1)
    send_chunk(0)
    send_chunk(1)
    for h, (x0, x1, x2, x3) in enumerate(quarter):
        put((x0 + x2) - (x1 + x3), 256 + h * 128)
    column_part(1)
    for h, (x0, x1, x2, x3) in enumerate(quarter):
        put(x0 - x2, 512 + h * 128)
        put(x1 - x3, 768 + h * 128)
    column_part(2)
    column_part(3)
    for p in range(4):
        rbuf[p, me] = sbuf[p, me]

    pltpu.make_async_copy(phase_v, phase_v, in_sem.at[2]).wait()
    cos_v[...] = jnp.cos(phase_v[...])
    sin_v[...] = jnp.sin(phase_v[...])
    pltpu.make_async_copy(lab_v, lab_v, in_sem.at[1]).wait()
    for p, v in enumerate(PARTS):
        reals, imags = [], []
        for k in range(PIX):
            for m in range(8):
                cosine = cos_v[m, pl.ds(v, ROWS, stride=4), :]
                sine = sin_v[m, pl.ds(v, ROWS, stride=4), :]
                zero = jnp.zeros_like(cosine)
                labels = lab_v[m, k, pl.ds(v, ROWS, stride=4), :]
                left = labels == 1
                right = labels == 2
                reals.append(jnp.where(left, cosine, jnp.where(right, -cosine, zero)))
                imags.append(jnp.where(jnp.logical_or(left, right), -sine, zero))
        for to, parts in ((wr, reals), (wi, imags)):
            for u1, part in enumerate(swap_bits(parts, (16, 8, 4, 2, 1))):
                to[p, u1] = part

    row_copy.wait()
    twiddle_copy.wait()

    def row_part(p):
        most = rbuf.at[p, pl.ds(0, SCAN - 1)]
        pltpu.make_async_copy(most, most, recv_sem.at[p]).wait()
        for e in range(4):
            points = [(rbuf[p, 4 * g + e, 0], rbuf[p, 4 * g + e, 1]) for g in range(8)]
            for b, point in enumerate(eight_points(points)):
                mixed[e, b, 0], mixed[e, b, 1] = turn(point, e * b)
        for b in range(8):
            points = four_points([(mixed[e, b, 0], mixed[e, b, 1]) for e in range(4)])
            for c, (re, im) in enumerate(points):
                u1 = b + 8 * c
                cosine, sine = twiddle_v[0, u1], twiddle_v[1, u1]
                turned[u1 * ROWS:(u1 + 1) * ROWS, :128] = re * cosine + im * sine
                turned[u1 * ROWS:(u1 + 1) * ROWS, 128:] = im * cosine - re * sine
        for qh in range(2):
            value = turned[qh * 128:(qh + 1) * 128]
            high = value.astype(BF16)
            lhs[qh, :128] = high
            lhs[qh, 128:] = (value - high.astype(F32)).astype(BF16)
            both = jnp.dot(lhs[qh], row_v[0], preferred_element_type=F32)
            low = jnp.dot(lhs[qh, :128], row_v[1], preferred_element_type=F32)
            spec = both[:128] + both[128:] + low
            sums = [], []
            for ql in range(4):
                reals, imags = [], []
                for e in range(4):
                    at = ql * 4 + e
                    re = spec[at * ROWS:(at + 1) * ROWS, :128]
                    im = spec[at * ROWS:(at + 1) * ROWS, 128:]
                    w_re, w_im = wr[p, qh * 16 + at], wi[p, qh * 16 + at]
                    reals.append(re * w_re - im * w_im)
                    imags.append(re * w_im + im * w_re)
                sums[0].append(sum_blocks(reals))
                sums[1].append(sum_blocks(imags))
            for e in range(2):
                for q, part in enumerate(swap_bits(sums[e], (4, 2))):
                    psend[p, q, qh, e] = part

        @pl.loop(1, X)
        def _(j):
            q = (x + j) % X
            pltpu.make_async_remote_copy(
                src_ref=psend.at[p, q],
                dst_ref=precv.at[p, j - 1],
                send_sem=psend_sem.at[p],
                recv_sem=precv_sem.at[p],
                device_id=(me, q * Z + z),
                device_id_type=MESH,
            ).start()

    def sum_x(p):
        pltpu.make_async_copy(precv.at[p], precv.at[p], precv_sem.at[p]).wait()
        parts = []
        for qh in range(2):
            for e in range(2):
                total = psend[p, x, qh, e]
                for j in range(X - 1):
                    total = total + precv[p, j, qh, e]
                parts.append(total)
        for h, part in enumerate(swap_bits(parts, (1, 64))):
            zsend[p, h] = part

        @pl.loop(1, Z)
        def _(j):
            to = (z + j) % Z
            pltpu.make_async_remote_copy(
                src_ref=zsend.at[p, to],
                dst_ref=zrecv.at[p, j - 1],
                send_sem=zsend_sem.at[p],
                recv_sem=zrecv_sem.at[p],
                device_id=(me, x * Z + to),
                device_id_type=MESH,
            ).start()

    @pl.loop(0, 8)
    def _(q):
        p = lax.div(q, 2)

        @pl.when(q < 6)
        def _():
            wait_sent(q)
            send_chunk(q + 2)

        @pl.when(lax.rem(q, 2) == 1)
        def _():
            @pl.when(jnp.logical_and(p > 0, p < 3))
            def _():
                sum_x(p - 1)

            row_part(p)

    sum_x(2)
    sum_x(3)

    lane = lax.broadcasted_iota(jnp.int32, (128, 128), 0)
    target = (
        lane // 32 * 32 + (lane % 2 * 4 + lane // 2 % 4) * 4 + lane // 8 % 4)
    order = jnp.where(
        target == lax.broadcasted_iota(jnp.int32, (128, 128), 1), 1.0, 0.0).astype(BF16)
    results = []
    for p in range(4):
        pltpu.make_async_copy(zrecv.at[p], zrecv.at[p], zrecv_sem.at[p]).wait()
        results.append(zsend[p, z] + zrecv[p, 0] + zrecv[p, 1] + zrecv[p, 2])
    result = jnp.concatenate(results, axis=0)
    moved = jnp.dot(jnp.concatenate(split3(result), axis=0), order, preferred_element_type=F32)
    result = moved[:BLOCK] + moved[BLOCK:2 * BLOCK] + moved[2 * BLOCK:]
    other = pltpu.roll(result, 64, 1)
    for p, v in enumerate(PARTS):
        o_v[0, pl.ds(v, ROWS, stride=4), :] = result[p * ROWS:(p + 1) * ROWS]
        o_v[1, pl.ds(v, ROWS, stride=4), :] = other[p * ROWS:(p + 1) * ROWS]
    o_ref[...] = o_v[:, :, :N // (X * Z)]

    for p in range(4):
        if p < 2:
            wait_sent(6 + p)
        pltpu.make_async_copy(precv.at[p], precv.at[p], psend_sem.at[p]).wait()
        pltpu.make_async_copy(zrecv.at[p], zrecv.at[p], zsend_sem.at[p]).wait()


def local(even, odd, row, twiddle, intensities, trotter_labels, phase_shift):
    any_spec = pl.BlockSpec(memory_space=pl.ANY)
    dma = pltpu.SemaphoreType.DMA
    return pl.pallas_call(
        kernel,
        out_shape=jax.ShapeDtypeStruct((2, BLOCK, N // (X * Z)), F32),
        in_specs=[any_spec] * 7,
        out_specs=pl.BlockSpec(memory_space=pltpu.VMEM),
        scratch_shapes=[
            pltpu.VMEM((PIX, BLOCK, N), F32),
            pltpu.VMEM((8, PIX, BLOCK, 128), jnp.int32),
            pltpu.VMEM((8, BLOCK, 128), F32),
            pltpu.VMEM((2, 1024, 256), BF16),
            pltpu.VMEM((2, 1024, 512), BF16),
            pltpu.VMEM((2, 256, 256), BF16),
            pltpu.VMEM((2, 32, ROWS, 128), F32),
            pltpu.VMEM((N, 256), BF16),
            pltpu.VMEM((4, SCAN, 2, ROWS, 128), F32),
            pltpu.VMEM((4, SCAN, 2, ROWS, 128), F32),
            pltpu.VMEM((4, 8, 2, ROWS, 128), F32),
            pltpu.VMEM((256, 256), F32),
            pltpu.VMEM((2, 256, 256), BF16),
            pltpu.VMEM((8, BLOCK, 128), F32),
            pltpu.VMEM((8, BLOCK, 128), F32),
            pltpu.VMEM((4, 32, ROWS, 128), F32),
            pltpu.VMEM((4, 32, ROWS, 128), F32),
            pltpu.VMEM((4, X, 2, 2, ROWS, 128), F32),
            pltpu.VMEM((4, X - 1, 2, 2, ROWS, 128), F32),
            pltpu.VMEM((4, Z, ROWS, 128), F32),
            pltpu.VMEM((4, Z - 1, ROWS, 128), F32),
            pltpu.VMEM((2, BLOCK, 128), F32),
            dma((10,)),
            dma((8,)),
            dma((4,)),
            dma((4,)),
            dma((4,)),
            dma((4,)),
            dma((4,)),
        ],
        compiler_params=pltpu.CompilerParams(
            collective_id=0, has_side_effects=True, vmem_limit_bytes=55140 * 1024),
        name="ptycho",
    )(intensities, trotter_labels, phase_shift, even, odd, row, twiddle)


def solution(mesh):
    tables = make_tables()
    placed = (P("det", "scan", None), P("det", "scan", None), P("scan", None))
    fixed = tuple(P(*[None] * table.ndim) for table in tables)
    mapped = jax.shard_map(
        local, mesh=mesh, in_specs=fixed + placed, out_specs=P(None, "scan", "det"),
        check_vma=False)

    def run(intensities, trotter_labels, phase_shift):
        return mapped(*map(jnp.asarray, tables), intensities, trotter_labels, phase_shift)

    return run
```

```python
import math

import jax
import jax.numpy as jnp
import ml_dtypes
import numpy as np
from jax import lax
from jax.experimental import pallas as pl
from jax.experimental.pallas import tpu as pltpu
from jax.sharding import PartitionSpec as P

MESH = pl.DeviceIdType.MESH
F32 = jnp.float32
BF16 = jnp.bfloat16

N = 1024
SCAN = 32
BLOCK = 32
PARTS = (0, 2, 1, 3)
ROWS = BLOCK // 4
PIX = 4
X = 4
Z = 4
FIRST = 1


def split_table(table):
    high = table.astype(ml_dtypes.bfloat16)
    low = (table - high.astype(np.float64)).astype(ml_dtypes.bfloat16)
    return high, low


def make_tables():
    index = np.arange(N)
    angles = (index[:, None] * index[None, :] % N) * (2.0 * math.pi / N)
    cosine, sine = np.cos(angles), np.sin(angles)
    cos_v = cosine[:, :256].reshape(SCAN, ROWS, 4, 256)
    sin_v = sine[:, :256].reshape(SCAN, ROWS, 4, 256)
    even, odd = [], []
    for v in PARTS:
        c, s = cos_v[:, :, v], sin_v[:, :, v]
        if v % 2 == 0:
            table = np.stack([c, -s], axis=1)
        else:
            sign = 1.0 if v == 3 else -1.0
            table = np.stack(
                [np.concatenate([c, sign * s], 2), np.concatenate([-s, sign * c], 2)], axis=1)
        table = np.concatenate(split_table(table.reshape(512, -1)), axis=0)
        (odd if v % 2 else even).append(table)
    twiddle = np.stack([cosine[:32, :32], sine[:32, :32]])
    twiddle = np.tile(twiddle, (1, 1, PIX)).astype(np.float32)[:, :, None]
    twiddle = np.repeat(twiddle, ROWS, axis=2)
    u2 = np.arange(32)
    lanes = ((u2 % 4) * 32 + u2 // 4)[None, :] + 8 * np.arange(PIX)[:, None]
    small = np.zeros((2, 128, 128))
    for k in range(PIX):
        for e, table in enumerate((cosine, sine)):
            small[e, k * 32:(k + 1) * 32, lanes[k]] = table[:32, 0:N:32].T
    row = np.block([[small[0], -small[1]], [small[1], small[0]]]) / (N * 8.0)
    row = np.stack(split_table(row))
    return np.stack(even), np.stack(odd), row, twiddle


def swap_bit(first, second, width):
    clear = lax.broadcasted_iota(jnp.int32, first.shape, 1) % (2 * width) < width
    return (
        jnp.where(clear, first, pltpu.roll(second, width, 1)),
        jnp.where(clear, pltpu.roll(first, 128 - width, 1), second),
    )


def swap_bits(parts, widths):
    parts = list(parts)
    step = len(parts)
    for width in widths:
        step //= 2
        for n in range(len(parts)):
            if n // step % 2 == 0:
                parts[n], parts[n + step] = swap_bit(parts[n], parts[n + step], width)
    return parts


def sum_blocks(parts):
    lane = lax.broadcasted_iota(jnp.int32, parts[0].shape, 1)
    for width in (16, 8):
        clear = lane % (2 * width) < width
        half = len(parts) // 2
        sums = []
        for one, two in zip(parts[:half], parts[half:]):
            other = jnp.where(clear, two, one)
            other = jnp.where(
                clear, pltpu.roll(other, 128 - width, 1), pltpu.roll(other, width, 1))
            sums.append(jnp.where(clear, one, two) + other)
        parts = sums
    return parts[0]


def four_points(p):
    (ar, ai), (br, bi), (cr, ci), (dr, di) = p
    sr, si, er, ei = ar + cr, ai + ci, ar - cr, ai - ci
    tr, ti, fr, fi = br + dr, bi + di, br - dr, bi - di
    return [(sr + tr, si + ti), (er + fi, ei - fr), (sr - tr, si - ti), (er - fi, ei + fr)]


def eight_points(p):
    root = math.sqrt(0.5)
    even = four_points(p[0::2])
    odd = four_points(p[1::2])
    (r1, i1), (r2, i2), (r3, i3) = odd[1:]
    odd[1] = ((r1 + i1) * root, (i1 - r1) * root)
    odd[2] = (i2, -r2)
    odd[3] = ((i3 - r3) * root, -(r3 + i3) * root)
    out = [(e[0] + o[0], e[1] + o[1]) for e, o in zip(even, odd)]
    return out + [(e[0] - o[0], e[1] - o[1]) for e, o in zip(even, odd)]


def turn(p, step):
    if step == 0:
        return p
    c, s = math.cos(2.0 * math.pi * step / 32), math.sin(2.0 * math.pi * step / 32)
    return p[0] * c + p[1] * s, p[1] * c - p[0] * s


def split3(value):
    high = value.astype(BF16)
    rest = value - high.astype(F32)
    middle = rest.astype(BF16)
    return high, middle, (rest - middle.astype(F32)).astype(BF16)


def kernel(
    x_hbm, lab_hbm, phase_hbm, even_hbm, odd_hbm, row_hbm, twiddle_hbm, o_ref,
    x_v, lab_v, phase_v, even_v, odd_v, row_v, twiddle_v,
    xt, sbuf, rbuf, mixed, turned, lhs, cos_v, sin_v,
    wr, wi, psend, precv, zsend, zrecv, o_v,
    in_sem, send_sem, recv_sem, psend_sem, precv_sem, zsend_sem, zrecv_sem,
):
    me = lax.axis_index("scan")
    det = lax.axis_index("det")
    x, z = det // Z, det % Z

    x_copy = pltpu.make_async_copy(x_hbm, x_v, in_sem.at[0])
    lab_copies = [
        pltpu.make_async_copy(
            lab_hbm.at[:, :, pl.ds(m * 128, 128)], lab_v.at[m], in_sem.at[1])
        for m in range(8)
    ]
    phase_copies = [
        pltpu.make_async_copy(phase_hbm.at[:, pl.ds(m * 128, 128)], phase_v.at[m], in_sem.at[2])
        for m in range(8)
    ]
    row_copy = pltpu.make_async_copy(row_hbm, row_v, in_sem.at[3])
    twiddle_copy = pltpu.make_async_copy(twiddle_hbm, twiddle_v, in_sem.at[4])
    col_copies = [
        pltpu.make_async_copy(table.at[p % 2], to.at[p % 2], in_sem.at[6 + p])
        for p, (table, to) in enumerate([(even_hbm, even_v)] * 2 + [(odd_hbm, odd_v)] * 2)
    ]

    x_copy.start()
    col_copies[0].start()

    barrier = pltpu.get_barrier_semaphore()

    for i in range(1, SCAN):
        pl.semaphore_signal(
            barrier, inc=1, device_id=(lax.rem(me + i, SCAN), det), device_id_type=MESH)

    for i in range(1, 4):
        pl.semaphore_signal(
            barrier, inc=1, device_id=(me, lax.rem(x + i, X) * Z + z), device_id_type=MESH)
        pl.semaphore_signal(
            barrier, inc=1, device_id=(me, x * Z + lax.rem(z + i, Z)), device_id_type=MESH)

    for p in range(1, 4):
        col_copies[p].start()
    for copy in lab_copies + phase_copies:
        copy.start()
    row_copy.start()
    twiddle_copy.start()

    x_copy.wait()
    quarter = [[x_v[:, :, q * 256 + h * 128:q * 256 + (h + 1) * 128].reshape(128, 128)
                for q in range(4)] for h in range(2)]

    def put(value, at):
        value = jnp.transpose(value)
        high = value.astype(BF16)
        xt[at:at + 128, :128] = high
        xt[at:at + 128, 128:] = (value - high.astype(F32)).astype(BF16)

    for h, (x0, x1, x2, x3) in enumerate(quarter):
        put((x0 + x2) + (x1 + x3), h * 128)

    def column_part(p):
        col_copies[p].wait()
        table = even_v if p < 2 else odd_v
        rows = xt[p * 256:(p + 1) * 256] if p < 2 else xt[512:]
        prod = jnp.dot(table[p % 2], rows, preferred_element_type=F32)
        top = prod[:512] + prod[512:]
        sbuf[p] = (top[:, :128] + top[:, 128:]).reshape(SCAN, 2, ROWS, 128)

    chip, own = lax.div(me, 2), lax.rem(me, 2)

    def send(p, to, q):
        pltpu.make_async_remote_copy(
            src_ref=sbuf.at[p, to],
            dst_ref=rbuf.at[p, me],
            send_sem=send_sem.at[jnp.minimum(q, 6)],
            recv_sem=recv_sem.at[p],
            device_id=(to, det),
            device_id_type=MESH,
        ).start()

    def send_chunk(q):
        p, core = lax.div(q, 2), lax.rem(q, 2)

        @pl.when(jnp.logical_and(q == 6, me != FIRST))
        def _():
            send(p, FIRST, q)

        @pl.loop(1, 17)
        def _(i):
            to = lax.rem(chip + i, 16) * 2 + core
            led = jnp.logical_and(p == 3, to == FIRST)

            @pl.when(jnp.logical_not(jnp.logical_or(to == me, led)))
            def _():
                send(p, to, q)

    def wait_sent(q):
        same = lax.rem(q, 2) == own
        for mine, count in ((same, 15), (jnp.logical_not(same), 16)):
            @pl.when(mine)
            def _(count=count):
                most = rbuf.at[0, pl.ds(0, count)]
                pltpu.make_async_copy(most, most, send_sem.at[q]).wait()

    column_part(0)
    pl.semaphore_wait(barrier, SCAN - 1 + X - 1 + Z - 1)
    send_chunk(0)
    send_chunk(1)
    for h, (x0, x1, x2, x3) in enumerate(quarter):
        put((x0 + x2) - (x1 + x3), 256 + h * 128)
    column_part(1)
    for h, (x0, x1, x2, x3) in enumerate(quarter):
        put(x0 - x2, 512 + h * 128)
        put(x1 - x3, 768 + h * 128)
    column_part(2)
    column_part(3)
    for p in range(4):
        rbuf[p, me] = sbuf[p, me]

    pltpu.make_async_copy(phase_v, phase_v, in_sem.at[2]).wait()
    cos_v[...] = jnp.cos(phase_v[...])
    sin_v[...] = jnp.sin(phase_v[...])
    pltpu.make_async_copy(lab_v, lab_v, in_sem.at[1]).wait()
    for p, v in enumerate(PARTS):
        reals, imags = [], []
        for k in range(PIX):
            for m in range(8):
                cosine = cos_v[m, pl.ds(v, ROWS, stride=4), :]
                sine = sin_v[m, pl.ds(v, ROWS, stride=4), :]
                zero = jnp.zeros_like(cosine)
                labels = lab_v[m, k, pl.ds(v, ROWS, stride=4), :]
                left = labels == 1
                right = labels == 2
                reals.append(jnp.where(left, cosine, jnp.where(right, -cosine, zero)))
                imags.append(jnp.where(jnp.logical_or(left, right), -sine, zero))
        for to, parts in ((wr, reals), (wi, imags)):
            for u1, part in enumerate(swap_bits(parts, (16, 8, 4, 2, 1))):
                to[p, u1] = part

    row_copy.wait()
    twiddle_copy.wait()

    def row_part(p):
        most = rbuf.at[p, pl.ds(0, SCAN - 1)]
        pltpu.make_async_copy(most, most, recv_sem.at[p]).wait()
        for e in range(4):
            points = [(rbuf[p, 4 * g + e, 0], rbuf[p, 4 * g + e, 1]) for g in range(8)]
            for b, point in enumerate(eight_points(points)):
                mixed[e, b, 0], mixed[e, b, 1] = turn(point, e * b)
        for b in range(8):
            points = four_points([(mixed[e, b, 0], mixed[e, b, 1]) for e in range(4)])
            for c, (re, im) in enumerate(points):
                u1 = b + 8 * c
                cosine, sine = twiddle_v[0, u1], twiddle_v[1, u1]
                turned[u1 * ROWS:(u1 + 1) * ROWS, :128] = re * cosine + im * sine
                turned[u1 * ROWS:(u1 + 1) * ROWS, 128:] = im * cosine - re * sine
        for qh in range(2):
            value = turned[qh * 128:(qh + 1) * 128]
            high = value.astype(BF16)
            lhs[qh, :128] = high
            lhs[qh, 128:] = (value - high.astype(F32)).astype(BF16)
            both = jnp.dot(lhs[qh], row_v[0], preferred_element_type=F32)
            low = jnp.dot(lhs[qh, :128], row_v[1], preferred_element_type=F32)
            spec = both[:128] + both[128:] + low
            sums = [], []
            for ql in range(4):
                reals, imags = [], []
                for e in range(4):
                    at = ql * 4 + e
                    re = spec[at * ROWS:(at + 1) * ROWS, :128]
                    im = spec[at * ROWS:(at + 1) * ROWS, 128:]
                    w_re, w_im = wr[p, qh * 16 + at], wi[p, qh * 16 + at]
                    reals.append(re * w_re - im * w_im)
                    imags.append(re * w_im + im * w_re)
                sums[0].append(sum_blocks(reals))
                sums[1].append(sum_blocks(imags))
            for e in range(2):
                for q, part in enumerate(swap_bits(sums[e], (4, 2))):
                    psend[p, q, qh, e] = part

        @pl.loop(1, X)
        def _(j):
            q = (x + j) % X
            pltpu.make_async_remote_copy(
                src_ref=psend.at[p, q],
                dst_ref=precv.at[p, j - 1],
                send_sem=psend_sem.at[p],
                recv_sem=precv_sem.at[p],
                device_id=(me, q * Z + z),
                device_id_type=MESH,
            ).start()

    def sum_x(p):
        pltpu.make_async_copy(precv.at[p], precv.at[p], precv_sem.at[p]).wait()
        parts = []
        for qh in range(2):
            for e in range(2):
                total = psend[p, x, qh, e]
                for j in range(X - 1):
                    total = total + precv[p, j, qh, e]
                parts.append(total)
        for h, part in enumerate(swap_bits(parts, (1, 64))):
            zsend[p, h] = part

        @pl.loop(1, Z)
        def _(j):
            to = (z + j) % Z
            pltpu.make_async_remote_copy(
                src_ref=zsend.at[p, to],
                dst_ref=zrecv.at[p, j - 1],
                send_sem=zsend_sem.at[p],
                recv_sem=zrecv_sem.at[p],
                device_id=(me, x * Z + to),
                device_id_type=MESH,
            ).start()

    @pl.loop(0, 8)
    def _(q):
        p = lax.div(q, 2)

        @pl.when(q < 6)
        def _():
            wait_sent(q)
            send_chunk(q + 2)

        @pl.when(lax.rem(q, 2) == 1)
        def _():
            @pl.when(jnp.logical_and(p > 0, p < 3))
            def _():
                sum_x(p - 1)

            row_part(p)

    sum_x(2)
    sum_x(3)

    lane = lax.broadcasted_iota(jnp.int32, (128, 128), 0)
    target = (
        lane // 32 * 32 + (lane % 2 * 4 + lane // 2 % 4) * 4 + lane // 8 % 4)
    order = jnp.where(
        target == lax.broadcasted_iota(jnp.int32, (128, 128), 1), 1.0, 0.0).astype(BF16)
    results = []
    for p in range(4):
        pltpu.make_async_copy(zrecv.at[p], zrecv.at[p], zrecv_sem.at[p]).wait()
        results.append(zsend[p, z] + zrecv[p, 0] + zrecv[p, 1] + zrecv[p, 2])
    result = jnp.concatenate(results, axis=0)
    moved = jnp.dot(jnp.concatenate(split3(result), axis=0), order, preferred_element_type=F32)
    result = moved[:BLOCK] + moved[BLOCK:2 * BLOCK] + moved[2 * BLOCK:]
    other = pltpu.roll(result, 64, 1)
    for p, v in enumerate(PARTS):
        o_v[0, pl.ds(v, ROWS, stride=4), :] = result[p * ROWS:(p + 1) * ROWS]
        o_v[1, pl.ds(v, ROWS, stride=4), :] = other[p * ROWS:(p + 1) * ROWS]
    o_ref[...] = o_v[:, :, :N // (X * Z)]

    for p in range(4):
        if p == 0:
            most = rbuf.at[0, pl.ds(0, SCAN - 1)]
            pltpu.make_async_copy(most, most, send_sem.at[6]).wait()
        pltpu.make_async_copy(precv.at[p], precv.at[p], psend_sem.at[p]).wait()
        pltpu.make_async_copy(zrecv.at[p], zrecv.at[p], zsend_sem.at[p]).wait()


def local(even, odd, row, twiddle, intensities, trotter_labels, phase_shift):
    any_spec = pl.BlockSpec(memory_space=pl.ANY)
    dma = pltpu.SemaphoreType.DMA
    return pl.pallas_call(
        kernel,
        out_shape=jax.ShapeDtypeStruct((2, BLOCK, N // (X * Z)), F32),
        in_specs=[any_spec] * 7,
        out_specs=pl.BlockSpec(memory_space=pltpu.VMEM),
        scratch_shapes=[
            pltpu.VMEM((PIX, BLOCK, N), F32),
            pltpu.VMEM((8, PIX, BLOCK, 128), jnp.int32),
            pltpu.VMEM((8, BLOCK, 128), F32),
            pltpu.VMEM((2, 1024, 256), BF16),
            pltpu.VMEM((2, 1024, 512), BF16),
            pltpu.VMEM((2, 256, 256), BF16),
            pltpu.VMEM((2, 32, ROWS, 128), F32),
            pltpu.VMEM((N, 256), BF16),
            pltpu.VMEM((4, SCAN, 2, ROWS, 128), F32),
            pltpu.VMEM((4, SCAN, 2, ROWS, 128), F32),
            pltpu.VMEM((4, 8, 2, ROWS, 128), F32),
            pltpu.VMEM((256, 256), F32),
            pltpu.VMEM((2, 256, 256), BF16),
            pltpu.VMEM((8, BLOCK, 128), F32),
            pltpu.VMEM((8, BLOCK, 128), F32),
            pltpu.VMEM((4, 32, ROWS, 128), F32),
            pltpu.VMEM((4, 32, ROWS, 128), F32),
            pltpu.VMEM((4, X, 2, 2, ROWS, 128), F32),
            pltpu.VMEM((4, X - 1, 2, 2, ROWS, 128), F32),
            pltpu.VMEM((4, Z, ROWS, 128), F32),
            pltpu.VMEM((4, Z - 1, ROWS, 128), F32),
            pltpu.VMEM((2, BLOCK, 128), F32),
            dma((10,)),
            dma((7,)),
            dma((4,)),
            dma((4,)),
            dma((4,)),
            dma((4,)),
            dma((4,)),
        ],
        compiler_params=pltpu.CompilerParams(
            collective_id=0, has_side_effects=True, vmem_limit_bytes=55140 * 1024),
        name="ptycho",
    )(intensities, trotter_labels, phase_shift, even, odd, row, twiddle)


def solution(mesh):
    tables = make_tables()
    placed = (P("det", "scan", None), P("det", "scan", None), P("scan", None))
    fixed = tuple(P(*[None] * table.ndim) for table in tables)
    mapped = jax.shard_map(
        local, mesh=mesh, in_specs=fixed + placed, out_specs=P(None, "scan", "det"),
        check_vma=False)

    def run(intensities, trotter_labels, phase_shift):
        return mapped(*map(jnp.asarray, tables), intensities, trotter_labels, phase_shift)

    return run
```

```python
import math

import jax
import jax.numpy as jnp
import ml_dtypes
import numpy as np
from jax import lax
from jax.experimental import pallas as pl
from jax.experimental.pallas import tpu as pltpu
from jax.sharding import PartitionSpec as P

MESH = pl.DeviceIdType.MESH
F32 = jnp.float32
BF16 = jnp.bfloat16

N = 1024
SCAN = 32
BLOCK = 32
PARTS = (0, 2, 1, 3)
ROWS = BLOCK // 4
PIX = 4
X = 4
Z = 4
FIRST = 1


def split_table(table):
    high = table.astype(ml_dtypes.bfloat16)
    low = (table - high.astype(np.float64)).astype(ml_dtypes.bfloat16)
    return high, low


def make_tables():
    index = np.arange(N)
    angles = (index[:, None] * index[None, :] % N) * (2.0 * math.pi / N)
    cosine, sine = np.cos(angles), np.sin(angles)
    cos_v = cosine[:, :256].reshape(SCAN, ROWS, 4, 256)
    sin_v = sine[:, :256].reshape(SCAN, ROWS, 4, 256)
    even, odd = [], []
    for v in PARTS:
        c, s = cos_v[:, :, v], sin_v[:, :, v]
        if v % 2 == 0:
            table = np.stack([c, -s], axis=1)
        else:
            sign = 1.0 if v == 3 else -1.0
            table = np.stack(
                [np.concatenate([c, sign * s], 2), np.concatenate([-s, sign * c], 2)], axis=1)
        table = np.concatenate(split_table(table.reshape(512, -1)), axis=0)
        (odd if v % 2 else even).append(table)
    twiddle = np.stack([cosine[:32, :32], sine[:32, :32]])
    twiddle = np.tile(twiddle, (1, 1, PIX)).astype(np.float32)[:, :, None]
    twiddle = np.repeat(twiddle, ROWS, axis=2)
    u2 = np.arange(32)
    lanes = ((u2 % 4) * 32 + u2 // 4)[None, :] + 8 * np.arange(PIX)[:, None]
    small = np.zeros((2, 128, 128))
    for k in range(PIX):
        for e, table in enumerate((cosine, sine)):
            small[e, k * 32:(k + 1) * 32, lanes[k]] = table[:32, 0:N:32].T
    row = np.block([[small[0], -small[1]], [small[1], small[0]]]) / (N * 8.0)
    row = np.stack(split_table(row))
    return np.stack(even), np.stack(odd), row, twiddle


def swap_bit(first, second, width):
    clear = lax.broadcasted_iota(jnp.int32, first.shape, 1) % (2 * width) < width
    return (
        jnp.where(clear, first, pltpu.roll(second, width, 1)),
        jnp.where(clear, pltpu.roll(first, 128 - width, 1), second),
    )


def swap_bits(parts, widths):
    parts = list(parts)
    step = len(parts)
    for width in widths:
        step //= 2
        for n in range(len(parts)):
            if n // step % 2 == 0:
                parts[n], parts[n + step] = swap_bit(parts[n], parts[n + step], width)
    return parts


def sum_blocks(parts):
    lane = lax.broadcasted_iota(jnp.int32, parts[0].shape, 1)
    for width in (16, 8):
        clear = lane % (2 * width) < width
        half = len(parts) // 2
        sums = []
        for one, two in zip(parts[:half], parts[half:]):
            other = jnp.where(clear, two, one)
            other = jnp.where(
                clear, pltpu.roll(other, 128 - width, 1), pltpu.roll(other, width, 1))
            sums.append(jnp.where(clear, one, two) + other)
        parts = sums
    return parts[0]


def four_points(p):
    (ar, ai), (br, bi), (cr, ci), (dr, di) = p
    sr, si, er, ei = ar + cr, ai + ci, ar - cr, ai - ci
    tr, ti, fr, fi = br + dr, bi + di, br - dr, bi - di
    return [(sr + tr, si + ti), (er + fi, ei - fr), (sr - tr, si - ti), (er - fi, ei + fr)]


def eight_points(p):
    root = math.sqrt(0.5)
    even = four_points(p[0::2])
    odd = four_points(p[1::2])
    (r1, i1), (r2, i2), (r3, i3) = odd[1:]
    odd[1] = ((r1 + i1) * root, (i1 - r1) * root)
    odd[2] = (i2, -r2)
    odd[3] = ((i3 - r3) * root, -(r3 + i3) * root)
    out = [(e[0] + o[0], e[1] + o[1]) for e, o in zip(even, odd)]
    return out + [(e[0] - o[0], e[1] - o[1]) for e, o in zip(even, odd)]


def turn(p, step):
    if step == 0:
        return p
    c, s = math.cos(2.0 * math.pi * step / 32), math.sin(2.0 * math.pi * step / 32)
    return p[0] * c + p[1] * s, p[1] * c - p[0] * s


def split3(value):
    high = value.astype(BF16)
    rest = value - high.astype(F32)
    middle = rest.astype(BF16)
    return high, middle, (rest - middle.astype(F32)).astype(BF16)


def kernel(
    x_hbm, lab_hbm, phase_hbm, even_hbm, odd_hbm, row_hbm, twiddle_hbm, o_ref,
    x_v, lab_v, phase_v, even_v, odd_v, row_v, twiddle_v,
    xt, sbuf, rbuf, mixed, turned, lhs, cos_v, sin_v,
    wr, wi, psend, precv, zsend, zrecv, o_v,
    in_sem, send_sem, recv_sem, psend_sem, precv_sem, zsend_sem, zrecv_sem,
):
    me = lax.axis_index("scan")
    det = lax.axis_index("det")
    x, z = det // Z, det % Z

    x_copy = pltpu.make_async_copy(x_hbm, x_v, in_sem.at[0])
    lab_copies = [
        pltpu.make_async_copy(
            lab_hbm.at[:, :, pl.ds(m * 128, 128)], lab_v.at[m], in_sem.at[1])
        for m in range(8)
    ]
    phase_copies = [
        pltpu.make_async_copy(phase_hbm.at[:, pl.ds(m * 128, 128)], phase_v.at[m], in_sem.at[2])
        for m in range(8)
    ]
    row_copy = pltpu.make_async_copy(row_hbm, row_v, in_sem.at[3])
    twiddle_copy = pltpu.make_async_copy(twiddle_hbm, twiddle_v, in_sem.at[4])
    col_copies = [
        pltpu.make_async_copy(table.at[p % 2], to.at[p % 2], in_sem.at[6 + p])
        for p, (table, to) in enumerate([(even_hbm, even_v)] * 2 + [(odd_hbm, odd_v)] * 2)
    ]

    x_copy.start()
    col_copies[0].start()

    barrier = pltpu.get_barrier_semaphore()

    for i in range(1, SCAN):
        pl.semaphore_signal(
            barrier, inc=1, device_id=(lax.rem(me + i, SCAN), det), device_id_type=MESH)

    for i in range(1, 4):
        pl.semaphore_signal(
            barrier, inc=1, device_id=(me, lax.rem(x + i, X) * Z + z), device_id_type=MESH)
        pl.semaphore_signal(
            barrier, inc=1, device_id=(me, x * Z + lax.rem(z + i, Z)), device_id_type=MESH)

    for p in range(1, 4):
        col_copies[p].start()
    for copy in lab_copies + phase_copies:
        copy.start()
    row_copy.start()
    twiddle_copy.start()

    x_copy.wait()
    quarter = [[x_v[:, :, q * 256 + h * 128:q * 256 + (h + 1) * 128].reshape(128, 128)
                for q in range(4)] for h in range(2)]

    def put(value, at):
        value = jnp.transpose(value)
        high = value.astype(BF16)
        xt[at:at + 128, :128] = high
        xt[at:at + 128, 128:] = (value - high.astype(F32)).astype(BF16)

    for h, (x0, x1, x2, x3) in enumerate(quarter):
        put((x0 + x2) + (x1 + x3), h * 128)

    def column_part(p):
        col_copies[p].wait()
        table = even_v if p < 2 else odd_v
        rows = xt[p * 256:(p + 1) * 256] if p < 2 else xt[512:]
        prod = jnp.dot(table[p % 2], rows, preferred_element_type=F32)
        top = prod[:512] + prod[512:]
        sbuf[p] = (top[:, :128] + top[:, 128:]).reshape(SCAN, 2, ROWS, 128)

    y, zl, own = lax.div(me, 8), lax.rem(lax.div(me, 2), 4), lax.rem(me, 2)

    def send(p, to, q):
        pltpu.make_async_remote_copy(
            src_ref=sbuf.at[p, to],
            dst_ref=rbuf.at[p, me],
            send_sem=send_sem.at[jnp.minimum(q, 6)],
            recv_sem=recv_sem.at[p],
            device_id=(to, det),
            device_id_type=MESH,
        ).start()

    def send_chunk(q):
        p, core = lax.div(q, 2), lax.rem(q, 2)

        @pl.when(jnp.logical_and(q == 6, me != FIRST))
        def _():
            send(p, FIRST, q)

        @pl.loop(0, 16)
        def _(i):
            to = lax.rem(y + lax.div(i, 4), 4) * 8 + lax.rem(zl + 1 + i, 4) * 2 + core
            led = jnp.logical_and(p == 3, to == FIRST)

            @pl.when(jnp.logical_not(jnp.logical_or(to == me, led)))
            def _():
                send(p, to, q)

    def wait_sent(q):
        same = lax.rem(q, 2) == own
        for mine, count in ((same, 15), (jnp.logical_not(same), 16)):
            @pl.when(mine)
            def _(count=count):
                most = rbuf.at[0, pl.ds(0, count)]
                pltpu.make_async_copy(most, most, send_sem.at[q]).wait()

    column_part(0)
    pl.semaphore_wait(barrier, SCAN - 1 + X - 1 + Z - 1)
    send_chunk(0)
    send_chunk(1)
    for h, (x0, x1, x2, x3) in enumerate(quarter):
        put((x0 + x2) - (x1 + x3), 256 + h * 128)
    column_part(1)
    for h, (x0, x1, x2, x3) in enumerate(quarter):
        put(x0 - x2, 512 + h * 128)
        put(x1 - x3, 768 + h * 128)
    column_part(2)
    column_part(3)
    for p in range(4):
        rbuf[p, me] = sbuf[p, me]

    pltpu.make_async_copy(phase_v, phase_v, in_sem.at[2]).wait()
    cos_v[...] = jnp.cos(phase_v[...])
    sin_v[...] = jnp.sin(phase_v[...])
    pltpu.make_async_copy(lab_v, lab_v, in_sem.at[1]).wait()
    for p, v in enumerate(PARTS):
        reals, imags = [], []
        for k in range(PIX):
            for m in range(8):
                cosine = cos_v[m, pl.ds(v, ROWS, stride=4), :]
                sine = sin_v[m, pl.ds(v, ROWS, stride=4), :]
                zero = jnp.zeros_like(cosine)
                labels = lab_v[m, k, pl.ds(v, ROWS, stride=4), :]
                left = labels == 1
                right = labels == 2
                reals.append(jnp.where(left, cosine, jnp.where(right, -cosine, zero)))
                imags.append(jnp.where(jnp.logical_or(left, right), -sine, zero))
        for to, parts in ((wr, reals), (wi, imags)):
            for u1, part in enumerate(swap_bits(parts, (16, 8, 4, 2, 1))):
                to[p, u1] = part

    row_copy.wait()
    twiddle_copy.wait()

    def row_part(p):
        most = rbuf.at[p, pl.ds(0, SCAN - 1)]
        pltpu.make_async_copy(most, most, recv_sem.at[p]).wait()
        for e in range(4):
            points = [(rbuf[p, 4 * g + e, 0], rbuf[p, 4 * g + e, 1]) for g in range(8)]
            for b, point in enumerate(eight_points(points)):
                mixed[e, b, 0], mixed[e, b, 1] = turn(point, e * b)
        for b in range(8):
            points = four_points([(mixed[e, b, 0], mixed[e, b, 1]) for e in range(4)])
            for c, (re, im) in enumerate(points):
                u1 = b + 8 * c
                cosine, sine = twiddle_v[0, u1], twiddle_v[1, u1]
                turned[u1 * ROWS:(u1 + 1) * ROWS, :128] = re * cosine + im * sine
                turned[u1 * ROWS:(u1 + 1) * ROWS, 128:] = im * cosine - re * sine
        for qh in range(2):
            value = turned[qh * 128:(qh + 1) * 128]
            high = value.astype(BF16)
            lhs[qh, :128] = high
            lhs[qh, 128:] = (value - high.astype(F32)).astype(BF16)
            both = jnp.dot(lhs[qh], row_v[0], preferred_element_type=F32)
            low = jnp.dot(lhs[qh, :128], row_v[1], preferred_element_type=F32)
            spec = both[:128] + both[128:] + low
            sums = [], []
            for ql in range(4):
                reals, imags = [], []
                for e in range(4):
                    at = ql * 4 + e
                    re = spec[at * ROWS:(at + 1) * ROWS, :128]
                    im = spec[at * ROWS:(at + 1) * ROWS, 128:]
                    w_re, w_im = wr[p, qh * 16 + at], wi[p, qh * 16 + at]
                    reals.append(re * w_re - im * w_im)
                    imags.append(re * w_im + im * w_re)
                sums[0].append(sum_blocks(reals))
                sums[1].append(sum_blocks(imags))
            for e in range(2):
                for q, part in enumerate(swap_bits(sums[e], (4, 2))):
                    psend[p, q, qh, e] = part

        @pl.loop(1, X)
        def _(j):
            q = (x + j) % X
            pltpu.make_async_remote_copy(
                src_ref=psend.at[p, q],
                dst_ref=precv.at[p, j - 1],
                send_sem=psend_sem.at[p],
                recv_sem=precv_sem.at[p],
                device_id=(me, q * Z + z),
                device_id_type=MESH,
            ).start()

    def sum_x(p):
        pltpu.make_async_copy(precv.at[p], precv.at[p], precv_sem.at[p]).wait()
        parts = []
        for qh in range(2):
            for e in range(2):
                total = psend[p, x, qh, e]
                for j in range(X - 1):
                    total = total + precv[p, j, qh, e]
                parts.append(total)
        for h, part in enumerate(swap_bits(parts, (1, 64))):
            zsend[p, h] = part

        @pl.loop(1, Z)
        def _(j):
            to = (z + j) % Z
            pltpu.make_async_remote_copy(
                src_ref=zsend.at[p, to],
                dst_ref=zrecv.at[p, j - 1],
                send_sem=zsend_sem.at[p],
                recv_sem=zrecv_sem.at[p],
                device_id=(me, x * Z + to),
                device_id_type=MESH,
            ).start()

    @pl.loop(0, 8)
    def _(q):
        p = lax.div(q, 2)

        @pl.when(q < 6)
        def _():
            wait_sent(q)
            send_chunk(q + 2)

        @pl.when(lax.rem(q, 2) == 1)
        def _():
            @pl.when(jnp.logical_and(p > 0, p < 3))
            def _():
                sum_x(p - 1)

            row_part(p)

    sum_x(2)
    sum_x(3)

    lane = lax.broadcasted_iota(jnp.int32, (128, 128), 0)
    target = (
        lane // 32 * 32 + (lane % 2 * 4 + lane // 2 % 4) * 4 + lane // 8 % 4)
    order = jnp.where(
        target == lax.broadcasted_iota(jnp.int32, (128, 128), 1), 1.0, 0.0).astype(BF16)
    results = []
    for p in range(4):
        pltpu.make_async_copy(zrecv.at[p], zrecv.at[p], zrecv_sem.at[p]).wait()
        results.append(zsend[p, z] + zrecv[p, 0] + zrecv[p, 1] + zrecv[p, 2])
    result = jnp.concatenate(results, axis=0)
    moved = jnp.dot(jnp.concatenate(split3(result), axis=0), order, preferred_element_type=F32)
    result = moved[:BLOCK] + moved[BLOCK:2 * BLOCK] + moved[2 * BLOCK:]
    other = pltpu.roll(result, 64, 1)
    for p, v in enumerate(PARTS):
        o_v[0, pl.ds(v, ROWS, stride=4), :] = result[p * ROWS:(p + 1) * ROWS]
        o_v[1, pl.ds(v, ROWS, stride=4), :] = other[p * ROWS:(p + 1) * ROWS]
    o_ref[...] = o_v[:, :, :N // (X * Z)]

    for p in range(4):
        if p == 0:
            most = rbuf.at[0, pl.ds(0, SCAN - 1)]
            pltpu.make_async_copy(most, most, send_sem.at[6]).wait()
        pltpu.make_async_copy(precv.at[p], precv.at[p], psend_sem.at[p]).wait()
        pltpu.make_async_copy(zrecv.at[p], zrecv.at[p], zsend_sem.at[p]).wait()


def local(even, odd, row, twiddle, intensities, trotter_labels, phase_shift):
    any_spec = pl.BlockSpec(memory_space=pl.ANY)
    dma = pltpu.SemaphoreType.DMA
    return pl.pallas_call(
        kernel,
        out_shape=jax.ShapeDtypeStruct((2, BLOCK, N // (X * Z)), F32),
        in_specs=[any_spec] * 7,
        out_specs=pl.BlockSpec(memory_space=pltpu.VMEM),
        scratch_shapes=[
            pltpu.VMEM((PIX, BLOCK, N), F32),
            pltpu.VMEM((8, PIX, BLOCK, 128), jnp.int32),
            pltpu.VMEM((8, BLOCK, 128), F32),
            pltpu.VMEM((2, 1024, 256), BF16),
            pltpu.VMEM((2, 1024, 512), BF16),
            pltpu.VMEM((2, 256, 256), BF16),
            pltpu.VMEM((2, 32, ROWS, 128), F32),
            pltpu.VMEM((N, 256), BF16),
            pltpu.VMEM((4, SCAN, 2, ROWS, 128), F32),
            pltpu.VMEM((4, SCAN, 2, ROWS, 128), F32),
            pltpu.VMEM((4, 8, 2, ROWS, 128), F32),
            pltpu.VMEM((256, 256), F32),
            pltpu.VMEM((2, 256, 256), BF16),
            pltpu.VMEM((8, BLOCK, 128), F32),
            pltpu.VMEM((8, BLOCK, 128), F32),
            pltpu.VMEM((4, 32, ROWS, 128), F32),
            pltpu.VMEM((4, 32, ROWS, 128), F32),
            pltpu.VMEM((4, X, 2, 2, ROWS, 128), F32),
            pltpu.VMEM((4, X - 1, 2, 2, ROWS, 128), F32),
            pltpu.VMEM((4, Z, ROWS, 128), F32),
            pltpu.VMEM((4, Z - 1, ROWS, 128), F32),
            pltpu.VMEM((2, BLOCK, 128), F32),
            dma((10,)),
            dma((7,)),
            dma((4,)),
            dma((4,)),
            dma((4,)),
            dma((4,)),
            dma((4,)),
        ],
        compiler_params=pltpu.CompilerParams(
            collective_id=0, has_side_effects=True, vmem_limit_bytes=55140 * 1024),
        name="ptycho",
    )(intensities, trotter_labels, phase_shift, even, odd, row, twiddle)


def solution(mesh):
    tables = make_tables()
    placed = (P("det", "scan", None), P("det", "scan", None), P("scan", None))
    fixed = tuple(P(*[None] * table.ndim) for table in tables)
    mapped = jax.shard_map(
        local, mesh=mesh, in_specs=fixed + placed, out_specs=P(None, "scan", "det"),
        check_vma=False)

    def run(intensities, trotter_labels, phase_shift):
        return mapped(*map(jnp.asarray, tables), intensities, trotter_labels, phase_shift)

    return run
```

```python
import math

import jax
import jax.numpy as jnp
import ml_dtypes
import numpy as np
from jax import lax
from jax.experimental import pallas as pl
from jax.experimental.pallas import tpu as pltpu
from jax.sharding import PartitionSpec as P

MESH = pl.DeviceIdType.MESH
F32 = jnp.float32
BF16 = jnp.bfloat16

N = 1024
SCAN = 32
BLOCK = 32
PARTS = (0, 2, 1, 3)
ROWS = BLOCK // 4
PIX = 4
X = 4
Z = 4
FIRST = 1


def split_table(table):
    high = table.astype(ml_dtypes.bfloat16)
    low = (table - high.astype(np.float64)).astype(ml_dtypes.bfloat16)
    return high, low


def make_tables():
    index = np.arange(N)
    angles = (index[:, None] * index[None, :] % N) * (2.0 * math.pi / N)
    cosine, sine = np.cos(angles), np.sin(angles)
    cos_v = cosine[:, :256].reshape(SCAN, ROWS, 4, 256)
    sin_v = sine[:, :256].reshape(SCAN, ROWS, 4, 256)
    even, odd = [], []
    for v in PARTS:
        c, s = cos_v[:, :, v], sin_v[:, :, v]
        if v % 2 == 0:
            table = np.stack([c, -s], axis=1)
        else:
            sign = 1.0 if v == 3 else -1.0
            table = np.stack(
                [np.concatenate([c, sign * s], 2), np.concatenate([-s, sign * c], 2)], axis=1)
        table = np.concatenate(split_table(table.reshape(512, -1)), axis=0)
        (odd if v % 2 else even).append(table)
    twiddle = np.stack([cosine[:32, :32], sine[:32, :32]])
    twiddle = np.tile(twiddle, (1, 1, PIX)).astype(np.float32)[:, :, None]
    twiddle = np.repeat(twiddle, ROWS, axis=2)
    u2 = np.arange(32)
    lanes = ((u2 % 4) * 32 + u2 // 4)[None, :] + 8 * np.arange(PIX)[:, None]
    small = np.zeros((2, 128, 128))
    for k in range(PIX):
        for e, table in enumerate((cosine, sine)):
            small[e, k * 32:(k + 1) * 32, lanes[k]] = table[:32, 0:N:32].T
    row = np.block([[small[0], -small[1]], [small[1], small[0]]]) / (N * 8.0)
    row = np.stack(split_table(row))
    return np.stack(even), np.stack(odd), row, twiddle


def swap_bit(first, second, width):
    clear = lax.broadcasted_iota(jnp.int32, first.shape, 1) % (2 * width) < width
    return (
        jnp.where(clear, first, pltpu.roll(second, width, 1)),
        jnp.where(clear, pltpu.roll(first, 128 - width, 1), second),
    )


def swap_bits(parts, widths):
    parts = list(parts)
    step = len(parts)
    for width in widths:
        step //= 2
        for n in range(len(parts)):
            if n // step % 2 == 0:
                parts[n], parts[n + step] = swap_bit(parts[n], parts[n + step], width)
    return parts


def sum_blocks(parts):
    lane = lax.broadcasted_iota(jnp.int32, parts[0].shape, 1)
    for width in (16, 8):
        clear = lane % (2 * width) < width
        half = len(parts) // 2
        sums = []
        for one, two in zip(parts[:half], parts[half:]):
            other = jnp.where(clear, two, one)
            other = jnp.where(
                clear, pltpu.roll(other, 128 - width, 1), pltpu.roll(other, width, 1))
            sums.append(jnp.where(clear, one, two) + other)
        parts = sums
    return parts[0]


def four_points(p):
    (ar, ai), (br, bi), (cr, ci), (dr, di) = p
    sr, si, er, ei = ar + cr, ai + ci, ar - cr, ai - ci
    tr, ti, fr, fi = br + dr, bi + di, br - dr, bi - di
    return [(sr + tr, si + ti), (er + fi, ei - fr), (sr - tr, si - ti), (er - fi, ei + fr)]


def eight_points(p):
    root = math.sqrt(0.5)
    even = four_points(p[0::2])
    odd = four_points(p[1::2])
    (r1, i1), (r2, i2), (r3, i3) = odd[1:]
    odd[1] = ((r1 + i1) * root, (i1 - r1) * root)
    odd[2] = (i2, -r2)
    odd[3] = ((i3 - r3) * root, -(r3 + i3) * root)
    out = [(e[0] + o[0], e[1] + o[1]) for e, o in zip(even, odd)]
    return out + [(e[0] - o[0], e[1] - o[1]) for e, o in zip(even, odd)]


def turn(p, step):
    if step == 0:
        return p
    c, s = math.cos(2.0 * math.pi * step / 32), math.sin(2.0 * math.pi * step / 32)
    return p[0] * c + p[1] * s, p[1] * c - p[0] * s


def split3(value):
    high = value.astype(BF16)
    rest = value - high.astype(F32)
    middle = rest.astype(BF16)
    return high, middle, (rest - middle.astype(F32)).astype(BF16)


def kernel(
    x_hbm, lab_hbm, phase_hbm, even_hbm, odd_hbm, row_hbm, twiddle_hbm, o_ref,
    x_v, lab_v, phase_v, even_v, odd_v, row_v, twiddle_v,
    xt, sbuf, rbuf, mixed, turned, lhs, cos_v, sin_v,
    wr, wi, psend, precv, zsend, zrecv, o_v,
    in_sem, send_sem, recv_sem, psend_sem, precv_sem, zsend_sem, zrecv_sem,
):
    me = lax.axis_index("scan")
    det = lax.axis_index("det")
    x, z = det // Z, det % Z

    x_copy = pltpu.make_async_copy(x_hbm, x_v, in_sem.at[0])
    lab_copies = [
        pltpu.make_async_copy(
            lab_hbm.at[:, :, pl.ds(m * 128, 128)], lab_v.at[m], in_sem.at[1])
        for m in range(8)
    ]
    phase_copies = [
        pltpu.make_async_copy(phase_hbm.at[:, pl.ds(m * 128, 128)], phase_v.at[m], in_sem.at[2])
        for m in range(8)
    ]
    row_copy = pltpu.make_async_copy(row_hbm, row_v, in_sem.at[3])
    twiddle_copy = pltpu.make_async_copy(twiddle_hbm, twiddle_v, in_sem.at[4])
    col_copies = [
        pltpu.make_async_copy(table.at[p % 2], to.at[p % 2], in_sem.at[6 + p])
        for p, (table, to) in enumerate([(even_hbm, even_v)] * 2 + [(odd_hbm, odd_v)] * 2)
    ]

    x_copy.start()
    col_copies[0].start()

    barrier = pltpu.get_barrier_semaphore()

    for i in range(1, SCAN):
        pl.semaphore_signal(
            barrier, inc=1, device_id=(lax.rem(me + i, SCAN), det), device_id_type=MESH)

    for i in range(1, 4):
        pl.semaphore_signal(
            barrier, inc=1, device_id=(me, lax.rem(x + i, X) * Z + z), device_id_type=MESH)
        pl.semaphore_signal(
            barrier, inc=1, device_id=(me, x * Z + lax.rem(z + i, Z)), device_id_type=MESH)

    for p in range(1, 4):
        col_copies[p].start()
    for copy in lab_copies + phase_copies:
        copy.start()
    row_copy.start()
    twiddle_copy.start()

    x_copy.wait()
    quarter = [[x_v[:, :, q * 256 + h * 128:q * 256 + (h + 1) * 128].reshape(128, 128)
                for q in range(4)] for h in range(2)]

    def put(value, at):
        value = jnp.transpose(value)
        high = value.astype(BF16)
        xt[at:at + 128, :128] = high
        xt[at:at + 128, 128:] = (value - high.astype(F32)).astype(BF16)

    for h, (x0, x1, x2, x3) in enumerate(quarter):
        put((x0 + x2) + (x1 + x3), h * 128)

    def column_part(p):
        col_copies[p].wait()
        table = even_v if p < 2 else odd_v
        rows = xt[p * 256:(p + 1) * 256] if p < 2 else xt[512:]
        prod = jnp.dot(table[p % 2], rows, preferred_element_type=F32)
        top = prod[:512] + prod[512:]
        sbuf[p] = (top[:, :128] + top[:, 128:]).reshape(SCAN, 2, ROWS, 128)

    chip, own = lax.div(me, 2), lax.rem(me, 2)

    def send(p, to, q):
        pltpu.make_async_remote_copy(
            src_ref=sbuf.at[p, to],
            dst_ref=rbuf.at[p, me],
            send_sem=send_sem.at[jnp.minimum(q, 6)],
            recv_sem=recv_sem.at[p],
            device_id=(to, det),
            device_id_type=MESH,
        ).start()

    def send_chunk(q):
        p, core = lax.div(q, 2), lax.rem(q, 2)

        @pl.when(jnp.logical_and(q == 6, me != FIRST))
        def _():
            send(p, FIRST, q)

        @pl.loop(1, 17)
        def _(i):
            to = lax.rem(chip + 8 * own + i, 16) * 2 + core
            led = jnp.logical_and(p == 3, to == FIRST)

            @pl.when(jnp.logical_not(jnp.logical_or(to == me, led)))
            def _():
                send(p, to, q)

    def wait_sent(q):
        same = lax.rem(q, 2) == own
        for mine, count in ((same, 15), (jnp.logical_not(same), 16)):
            @pl.when(mine)
            def _(count=count):
                most = rbuf.at[0, pl.ds(0, count)]
                pltpu.make_async_copy(most, most, send_sem.at[q]).wait()

    column_part(0)
    pl.semaphore_wait(barrier, SCAN - 1 + X - 1 + Z - 1)
    send_chunk(0)
    send_chunk(1)
    for h, (x0, x1, x2, x3) in enumerate(quarter):
        put((x0 + x2) - (x1 + x3), 256 + h * 128)
    column_part(1)
    for h, (x0, x1, x2, x3) in enumerate(quarter):
        put(x0 - x2, 512 + h * 128)
        put(x1 - x3, 768 + h * 128)
    column_part(2)
    column_part(3)
    for p in range(4):
        rbuf[p, me] = sbuf[p, me]

    pltpu.make_async_copy(phase_v, phase_v, in_sem.at[2]).wait()
    cos_v[...] = jnp.cos(phase_v[...])
    sin_v[...] = jnp.sin(phase_v[...])
    pltpu.make_async_copy(lab_v, lab_v, in_sem.at[1]).wait()
    for p, v in enumerate(PARTS):
        reals, imags = [], []
        for k in range(PIX):
            for m in range(8):
                cosine = cos_v[m, pl.ds(v, ROWS, stride=4), :]
                sine = sin_v[m, pl.ds(v, ROWS, stride=4), :]
                zero = jnp.zeros_like(cosine)
                labels = lab_v[m, k, pl.ds(v, ROWS, stride=4), :]
                left = labels == 1
                right = labels == 2
                reals.append(jnp.where(left, cosine, jnp.where(right, -cosine, zero)))
                imags.append(jnp.where(jnp.logical_or(left, right), -sine, zero))
        for to, parts in ((wr, reals), (wi, imags)):
            for u1, part in enumerate(swap_bits(parts, (16, 8, 4, 2, 1))):
                to[p, u1] = part

    row_copy.wait()
    twiddle_copy.wait()

    def row_part(p):
        most = rbuf.at[p, pl.ds(0, SCAN - 1)]
        pltpu.make_async_copy(most, most, recv_sem.at[p]).wait()
        for e in range(4):
            points = [(rbuf[p, 4 * g + e, 0], rbuf[p, 4 * g + e, 1]) for g in range(8)]
            for b, point in enumerate(eight_points(points)):
                mixed[e, b, 0], mixed[e, b, 1] = turn(point, e * b)
        for b in range(8):
            points = four_points([(mixed[e, b, 0], mixed[e, b, 1]) for e in range(4)])
            for c, (re, im) in enumerate(points):
                u1 = b + 8 * c
                cosine, sine = twiddle_v[0, u1], twiddle_v[1, u1]
                turned[u1 * ROWS:(u1 + 1) * ROWS, :128] = re * cosine + im * sine
                turned[u1 * ROWS:(u1 + 1) * ROWS, 128:] = im * cosine - re * sine
        for qh in range(2):
            value = turned[qh * 128:(qh + 1) * 128]
            high = value.astype(BF16)
            lhs[qh, :128] = high
            lhs[qh, 128:] = (value - high.astype(F32)).astype(BF16)
            both = jnp.dot(lhs[qh], row_v[0], preferred_element_type=F32)
            low = jnp.dot(lhs[qh, :128], row_v[1], preferred_element_type=F32)
            spec = both[:128] + both[128:] + low
            sums = [], []
            for ql in range(4):
                reals, imags = [], []
                for e in range(4):
                    at = ql * 4 + e
                    re = spec[at * ROWS:(at + 1) * ROWS, :128]
                    im = spec[at * ROWS:(at + 1) * ROWS, 128:]
                    w_re, w_im = wr[p, qh * 16 + at], wi[p, qh * 16 + at]
                    reals.append(re * w_re - im * w_im)
                    imags.append(re * w_im + im * w_re)
                sums[0].append(sum_blocks(reals))
                sums[1].append(sum_blocks(imags))
            for e in range(2):
                for q, part in enumerate(swap_bits(sums[e], (4, 2))):
                    psend[p, q, qh, e] = part

        @pl.loop(1, X)
        def _(j):
            q = (x + j) % X
            pltpu.make_async_remote_copy(
                src_ref=psend.at[p, q],
                dst_ref=precv.at[p, j - 1],
                send_sem=psend_sem.at[p],
                recv_sem=precv_sem.at[p],
                device_id=(me, q * Z + z),
                device_id_type=MESH,
            ).start()

    def sum_x(p):
        pltpu.make_async_copy(precv.at[p], precv.at[p], precv_sem.at[p]).wait()
        parts = []
        for qh in range(2):
            for e in range(2):
                total = psend[p, x, qh, e]
                for j in range(X - 1):
                    total = total + precv[p, j, qh, e]
                parts.append(total)
        for h, part in enumerate(swap_bits(parts, (1, 64))):
            zsend[p, h] = part

        @pl.loop(1, Z)
        def _(j):
            to = (z + j) % Z
            pltpu.make_async_remote_copy(
                src_ref=zsend.at[p, to],
                dst_ref=zrecv.at[p, j - 1],
                send_sem=zsend_sem.at[p],
                recv_sem=zrecv_sem.at[p],
                device_id=(me, x * Z + to),
                device_id_type=MESH,
            ).start()

    @pl.loop(0, 8)
    def _(q):
        p = lax.div(q, 2)

        @pl.when(q < 6)
        def _():
            wait_sent(q)
            send_chunk(q + 2)

        @pl.when(lax.rem(q, 2) == 1)
        def _():
            @pl.when(jnp.logical_and(p > 0, p < 3))
            def _():
                sum_x(p - 1)

            row_part(p)

    sum_x(2)
    sum_x(3)

    lane = lax.broadcasted_iota(jnp.int32, (128, 128), 0)
    target = (
        lane // 32 * 32 + (lane % 2 * 4 + lane // 2 % 4) * 4 + lane // 8 % 4)
    order = jnp.where(
        target == lax.broadcasted_iota(jnp.int32, (128, 128), 1), 1.0, 0.0).astype(BF16)
    results = []
    for p in range(4):
        pltpu.make_async_copy(zrecv.at[p], zrecv.at[p], zrecv_sem.at[p]).wait()
        results.append(zsend[p, z] + zrecv[p, 0] + zrecv[p, 1] + zrecv[p, 2])
    result = jnp.concatenate(results, axis=0)
    moved = jnp.dot(jnp.concatenate(split3(result), axis=0), order, preferred_element_type=F32)
    result = moved[:BLOCK] + moved[BLOCK:2 * BLOCK] + moved[2 * BLOCK:]
    other = pltpu.roll(result, 64, 1)
    for p, v in enumerate(PARTS):
        o_v[0, pl.ds(v, ROWS, stride=4), :] = result[p * ROWS:(p + 1) * ROWS]
        o_v[1, pl.ds(v, ROWS, stride=4), :] = other[p * ROWS:(p + 1) * ROWS]
    o_ref[...] = o_v[:, :, :N // (X * Z)]

    for p in range(4):
        if p == 0:
            most = rbuf.at[0, pl.ds(0, SCAN - 1)]
            pltpu.make_async_copy(most, most, send_sem.at[6]).wait()
        pltpu.make_async_copy(precv.at[p], precv.at[p], psend_sem.at[p]).wait()
        pltpu.make_async_copy(zrecv.at[p], zrecv.at[p], zsend_sem.at[p]).wait()


def local(even, odd, row, twiddle, intensities, trotter_labels, phase_shift):
    any_spec = pl.BlockSpec(memory_space=pl.ANY)
    dma = pltpu.SemaphoreType.DMA
    return pl.pallas_call(
        kernel,
        out_shape=jax.ShapeDtypeStruct((2, BLOCK, N // (X * Z)), F32),
        in_specs=[any_spec] * 7,
        out_specs=pl.BlockSpec(memory_space=pltpu.VMEM),
        scratch_shapes=[
            pltpu.VMEM((PIX, BLOCK, N), F32),
            pltpu.VMEM((8, PIX, BLOCK, 128), jnp.int32),
            pltpu.VMEM((8, BLOCK, 128), F32),
            pltpu.VMEM((2, 1024, 256), BF16),
            pltpu.VMEM((2, 1024, 512), BF16),
            pltpu.VMEM((2, 256, 256), BF16),
            pltpu.VMEM((2, 32, ROWS, 128), F32),
            pltpu.VMEM((N, 256), BF16),
            pltpu.VMEM((4, SCAN, 2, ROWS, 128), F32),
            pltpu.VMEM((4, SCAN, 2, ROWS, 128), F32),
            pltpu.VMEM((4, 8, 2, ROWS, 128), F32),
            pltpu.VMEM((256, 256), F32),
            pltpu.VMEM((2, 256, 256), BF16),
            pltpu.VMEM((8, BLOCK, 128), F32),
            pltpu.VMEM((8, BLOCK, 128), F32),
            pltpu.VMEM((4, 32, ROWS, 128), F32),
            pltpu.VMEM((4, 32, ROWS, 128), F32),
            pltpu.VMEM((4, X, 2, 2, ROWS, 128), F32),
            pltpu.VMEM((4, X - 1, 2, 2, ROWS, 128), F32),
            pltpu.VMEM((4, Z, ROWS, 128), F32),
            pltpu.VMEM((4, Z - 1, ROWS, 128), F32),
            pltpu.VMEM((2, BLOCK, 128), F32),
            dma((10,)),
            dma((7,)),
            dma((4,)),
            dma((4,)),
            dma((4,)),
            dma((4,)),
            dma((4,)),
        ],
        compiler_params=pltpu.CompilerParams(
            collective_id=0, has_side_effects=True, vmem_limit_bytes=55140 * 1024),
        name="ptycho",
    )(intensities, trotter_labels, phase_shift, even, odd, row, twiddle)


def solution(mesh):
    tables = make_tables()
    placed = (P("det", "scan", None), P("det", "scan", None), P("scan", None))
    fixed = tuple(P(*[None] * table.ndim) for table in tables)
    mapped = jax.shard_map(
        local, mesh=mesh, in_specs=fixed + placed, out_specs=P(None, "scan", "det"),
        check_vma=False)

    def run(intensities, trotter_labels, phase_shift):
        return mapped(*map(jnp.asarray, tables), intensities, trotter_labels, phase_shift)

    return run
```

```python
import math

import jax
import jax.numpy as jnp
import ml_dtypes
import numpy as np
from jax import lax
from jax.experimental import pallas as pl
from jax.experimental.pallas import tpu as pltpu
from jax.sharding import PartitionSpec as P

MESH = pl.DeviceIdType.MESH
F32 = jnp.float32
BF16 = jnp.bfloat16

N = 1024
SCAN = 32
BLOCK = 32
PARTS = (0, 2, 1, 3)
ROWS = BLOCK // 4
PIX = 4
X = 4
Z = 4
FIRST = 1


def split_table(table):
    high = table.astype(ml_dtypes.bfloat16)
    low = (table - high.astype(np.float64)).astype(ml_dtypes.bfloat16)
    return high, low


def make_tables():
    index = np.arange(N)
    angles = (index[:, None] * index[None, :] % N) * (2.0 * math.pi / N)
    cosine, sine = np.cos(angles), np.sin(angles)
    cos_v = cosine[:, :256].reshape(SCAN, ROWS, 4, 256)
    sin_v = sine[:, :256].reshape(SCAN, ROWS, 4, 256)
    even, odd = [], []
    for v in PARTS:
        c, s = cos_v[:, :, v], sin_v[:, :, v]
        if v % 2 == 0:
            table = np.stack([c, -s], axis=1)
        else:
            sign = 1.0 if v == 3 else -1.0
            table = np.stack(
                [np.concatenate([c, sign * s], 2), np.concatenate([-s, sign * c], 2)], axis=1)
        table = np.concatenate(split_table(table.reshape(512, -1)), axis=0)
        (odd if v % 2 else even).append(table)
    twiddle = np.stack([cosine[:32, :32], sine[:32, :32]])
    twiddle = np.tile(twiddle, (1, 1, PIX)).astype(np.float32)[:, :, None]
    twiddle = np.repeat(twiddle, ROWS, axis=2)
    u2 = np.arange(32)
    lanes = ((u2 % 4) * 32 + u2 // 4)[None, :] + 8 * np.arange(PIX)[:, None]
    small = np.zeros((2, 128, 128))
    for k in range(PIX):
        for e, table in enumerate((cosine, sine)):
            small[e, k * 32:(k + 1) * 32, lanes[k]] = table[:32, 0:N:32].T
    row = np.block([[small[0], -small[1]], [small[1], small[0]]]) / (N * 8.0)
    row = np.stack(split_table(row))
    return np.stack(even), np.stack(odd), row, twiddle


def swap_bit(first, second, width):
    clear = lax.broadcasted_iota(jnp.int32, first.shape, 1) % (2 * width) < width
    return (
        jnp.where(clear, first, pltpu.roll(second, width, 1)),
        jnp.where(clear, pltpu.roll(first, 128 - width, 1), second),
    )


def swap_bits(parts, widths):
    parts = list(parts)
    step = len(parts)
    for width in widths:
        step //= 2
        for n in range(len(parts)):
            if n // step % 2 == 0:
                parts[n], parts[n + step] = swap_bit(parts[n], parts[n + step], width)
    return parts


def sum_blocks(parts):
    lane = lax.broadcasted_iota(jnp.int32, parts[0].shape, 1)
    for width in (16, 8):
        clear = lane % (2 * width) < width
        half = len(parts) // 2
        sums = []
        for one, two in zip(parts[:half], parts[half:]):
            other = jnp.where(clear, two, one)
            other = jnp.where(
                clear, pltpu.roll(other, 128 - width, 1), pltpu.roll(other, width, 1))
            sums.append(jnp.where(clear, one, two) + other)
        parts = sums
    return parts[0]


def four_points(p):
    (ar, ai), (br, bi), (cr, ci), (dr, di) = p
    sr, si, er, ei = ar + cr, ai + ci, ar - cr, ai - ci
    tr, ti, fr, fi = br + dr, bi + di, br - dr, bi - di
    return [(sr + tr, si + ti), (er + fi, ei - fr), (sr - tr, si - ti), (er - fi, ei + fr)]


def eight_points(p):
    root = math.sqrt(0.5)
    even = four_points(p[0::2])
    odd = four_points(p[1::2])
    (r1, i1), (r2, i2), (r3, i3) = odd[1:]
    odd[1] = ((r1 + i1) * root, (i1 - r1) * root)
    odd[2] = (i2, -r2)
    odd[3] = ((i3 - r3) * root, -(r3 + i3) * root)
    out = [(e[0] + o[0], e[1] + o[1]) for e, o in zip(even, odd)]
    return out + [(e[0] - o[0], e[1] - o[1]) for e, o in zip(even, odd)]


def turn(p, step):
    if step == 0:
        return p
    c, s = math.cos(2.0 * math.pi * step / 32), math.sin(2.0 * math.pi * step / 32)
    return p[0] * c + p[1] * s, p[1] * c - p[0] * s


def split3(value):
    high = value.astype(BF16)
    rest = value - high.astype(F32)
    middle = rest.astype(BF16)
    return high, middle, (rest - middle.astype(F32)).astype(BF16)


def kernel(
    x_hbm, lab_hbm, phase_hbm, even_hbm, odd_hbm, row_hbm, twiddle_hbm, o_ref,
    x_v, lab_v, phase_v, even_v, odd_v, row_v, twiddle_v,
    xt, sbuf, rbuf, mixed, turned, lhs, cos_v, sin_v,
    wr, wi, psend, precv, zsend, zrecv, o_v,
    in_sem, send_sem, recv_sem, psend_sem, precv_sem, zsend_sem, zrecv_sem,
):
    me = lax.axis_index("scan")
    det = lax.axis_index("det")
    x, z = det // Z, det % Z

    x_copy = pltpu.make_async_copy(x_hbm, x_v, in_sem.at[0])
    lab_copies = [
        pltpu.make_async_copy(
            lab_hbm.at[:, :, pl.ds(m * 128, 128)], lab_v.at[m], in_sem.at[1])
        for m in range(8)
    ]
    phase_copies = [
        pltpu.make_async_copy(phase_hbm.at[:, pl.ds(m * 128, 128)], phase_v.at[m], in_sem.at[2])
        for m in range(8)
    ]
    row_copy = pltpu.make_async_copy(row_hbm, row_v, in_sem.at[3])
    twiddle_copy = pltpu.make_async_copy(twiddle_hbm, twiddle_v, in_sem.at[4])
    col_copies = [
        pltpu.make_async_copy(table.at[p % 2], to.at[p % 2], in_sem.at[6 + p])
        for p, (table, to) in enumerate([(even_hbm, even_v)] * 2 + [(odd_hbm, odd_v)] * 2)
    ]

    x_copy.start()
    col_copies[0].start()

    barrier = pltpu.get_barrier_semaphore()

    for i in range(1, SCAN):
        pl.semaphore_signal(
            barrier, inc=1, device_id=(lax.rem(me + i, SCAN), det), device_id_type=MESH)

    for i in range(1, 4):
        pl.semaphore_signal(
            barrier, inc=1, device_id=(me, lax.rem(x + i, X) * Z + z), device_id_type=MESH)
        pl.semaphore_signal(
            barrier, inc=1, device_id=(me, x * Z + lax.rem(z + i, Z)), device_id_type=MESH)

    for p in range(1, 4):
        col_copies[p].start()
    for copy in lab_copies + phase_copies:
        copy.start()
    row_copy.start()
    twiddle_copy.start()

    x_copy.wait()
    quarter = [[x_v[:, :, q * 256 + h * 128:q * 256 + (h + 1) * 128].reshape(128, 128)
                for q in range(4)] for h in range(2)]

    def put(value, at):
        value = jnp.transpose(value)
        high = value.astype(BF16)
        xt[at:at + 128, :128] = high
        xt[at:at + 128, 128:] = (value - high.astype(F32)).astype(BF16)

    for h, (x0, x1, x2, x3) in enumerate(quarter):
        put((x0 + x2) + (x1 + x3), h * 128)

    def column_part(p):
        col_copies[p].wait()
        table = even_v if p < 2 else odd_v
        rows = xt[p * 256:(p + 1) * 256] if p < 2 else xt[512:]
        prod = jnp.dot(table[p % 2], rows, preferred_element_type=F32)
        top = prod[:512] + prod[512:]
        sbuf[p] = (top[:, :128] + top[:, 128:]).reshape(SCAN, 2, ROWS, 128)

    chip, own = lax.div(me, 2), lax.rem(me, 2)

    def send(p, to, q):
        pltpu.make_async_remote_copy(
            src_ref=sbuf.at[p, to],
            dst_ref=rbuf.at[p, me],
            send_sem=send_sem.at[jnp.minimum(q, 6)],
            recv_sem=recv_sem.at[p],
            device_id=(to, det),
            device_id_type=MESH,
        ).start()

    def send_chunk(q):
        p, core = lax.div(q, 2), lax.rem(q, 2)

        @pl.when(jnp.logical_and(q == 6, me != FIRST))
        def _():
            send(p, FIRST, q)

        @pl.loop(1, 17)
        def _(i):
            to = lax.rem(chip + 8 * own + i, 16) * 2 + core
            led = jnp.logical_and(p == 3, to == FIRST)

            @pl.when(jnp.logical_not(jnp.logical_or(to == me, led)))
            def _():
                send(p, to, q)

    def wait_sent(q):
        same = lax.rem(q, 2) == own
        for mine, count in ((same, 15), (jnp.logical_not(same), 16)):
            @pl.when(mine)
            def _(count=count):
                most = rbuf.at[0, pl.ds(0, count)]
                pltpu.make_async_copy(most, most, send_sem.at[q]).wait()

    column_part(0)
    pl.semaphore_wait(barrier, SCAN - 1 + X - 1 + Z - 1)
    send_chunk(0)
    send_chunk(1)
    for h, (x0, x1, x2, x3) in enumerate(quarter):
        put((x0 + x2) - (x1 + x3), 256 + h * 128)
    column_part(1)
    for h, (x0, x1, x2, x3) in enumerate(quarter):
        put(x0 - x2, 512 + h * 128)
        put(x1 - x3, 768 + h * 128)
    column_part(2)
    column_part(3)
    for p in range(4):
        rbuf[p, me] = sbuf[p, me]

    pltpu.make_async_copy(phase_v, phase_v, in_sem.at[2]).wait()
    cos_v[...] = jnp.cos(phase_v[...])
    sin_v[...] = jnp.sin(phase_v[...])
    pltpu.make_async_copy(lab_v, lab_v, in_sem.at[1]).wait()
    for p, v in enumerate(PARTS):
        reals, imags = [], []
        for k in range(PIX):
            for m in range(8):
                cosine = cos_v[m, pl.ds(v, ROWS, stride=4), :]
                sine = sin_v[m, pl.ds(v, ROWS, stride=4), :]
                zero = jnp.zeros_like(cosine)
                labels = lab_v[m, k, pl.ds(v, ROWS, stride=4), :]
                left = labels == 1
                right = labels == 2
                reals.append(jnp.where(left, cosine, jnp.where(right, -cosine, zero)))
                imags.append(jnp.where(jnp.logical_or(left, right), -sine, zero))
        for to, parts in ((wr, reals), (wi, imags)):
            for u1, part in enumerate(swap_bits(parts, (16, 8, 4, 2, 1))):
                to[p, u1] = part

    row_copy.wait()
    twiddle_copy.wait()

    def row_part(p):
        most = rbuf.at[p, pl.ds(0, SCAN - 1)]
        pltpu.make_async_copy(most, most, recv_sem.at[p]).wait()
        for e in range(4):
            points = [(rbuf[p, 4 * g + e, 0], rbuf[p, 4 * g + e, 1]) for g in range(8)]
            for b, point in enumerate(eight_points(points)):
                mixed[e, b, 0], mixed[e, b, 1] = turn(point, e * b)
        for b in range(8):
            points = four_points([(mixed[e, b, 0], mixed[e, b, 1]) for e in range(4)])
            for c, (re, im) in enumerate(points):
                u1 = b + 8 * c
                cosine, sine = twiddle_v[0, u1], twiddle_v[1, u1]
                turned[u1 * ROWS:(u1 + 1) * ROWS, :128] = re * cosine + im * sine
                turned[u1 * ROWS:(u1 + 1) * ROWS, 128:] = im * cosine - re * sine
        for qh in range(2):
            value = turned[qh * 128:(qh + 1) * 128]
            high = value.astype(BF16)
            lhs[qh, :128] = high
            lhs[qh, 128:] = (value - high.astype(F32)).astype(BF16)
            both = jnp.dot(lhs[qh], row_v[0], preferred_element_type=F32)
            low = jnp.dot(lhs[qh, :128], row_v[1], preferred_element_type=F32)
            spec = both[:128] + both[128:] + low
            sums = [], []
            for ql in range(4):
                reals, imags = [], []
                for e in range(4):
                    at = ql * 4 + e
                    re = spec[at * ROWS:(at + 1) * ROWS, :128]
                    im = spec[at * ROWS:(at + 1) * ROWS, 128:]
                    w_re, w_im = wr[p, qh * 16 + at], wi[p, qh * 16 + at]
                    reals.append(re * w_re - im * w_im)
                    imags.append(re * w_im + im * w_re)
                sums[0].append(sum_blocks(reals))
                sums[1].append(sum_blocks(imags))
            for e in range(2):
                for q, part in enumerate(swap_bits(sums[e], (4, 2))):
                    psend[p, q, qh, e] = part

            for j in range(1, X):
                q = lax.rem(x + j, X)
                pltpu.make_async_remote_copy(
                    src_ref=psend.at[p, q, qh],
                    dst_ref=precv.at[p, j - 1, qh],
                    send_sem=psend_sem.at[p],
                    recv_sem=precv_sem.at[p],
                    device_id=(me, q * Z + z),
                    device_id_type=MESH,
                ).start()

    def sum_x(p):
        pltpu.make_async_copy(precv.at[p], precv.at[p], precv_sem.at[p]).wait()
        parts = []
        for qh in range(2):
            for e in range(2):
                total = psend[p, x, qh, e]
                for j in range(X - 1):
                    total = total + precv[p, j, qh, e]
                parts.append(total)
        for h, part in enumerate(swap_bits(parts, (1, 64))):
            zsend[p, h] = part

        @pl.loop(1, Z)
        def _(j):
            to = (z + j) % Z
            pltpu.make_async_remote_copy(
                src_ref=zsend.at[p, to],
                dst_ref=zrecv.at[p, j - 1],
                send_sem=zsend_sem.at[p],
                recv_sem=zrecv_sem.at[p],
                device_id=(me, x * Z + to),
                device_id_type=MESH,
            ).start()

    @pl.loop(0, 8)
    def _(q):
        p = lax.div(q, 2)

        @pl.when(q < 6)
        def _():
            wait_sent(q)

        @pl.when(jnp.logical_or(q == 3, q == 5))
        def _():
            sum_x(p - 1)

        @pl.when(q < 6)
        def _():
            send_chunk(q + 2)

        @pl.when(lax.rem(q, 2) == 1)
        def _():
            row_part(p)

    sum_x(2)
    sum_x(3)

    lane = lax.broadcasted_iota(jnp.int32, (128, 128), 0)
    target = (
        lane // 32 * 32 + (lane % 2 * 4 + lane // 2 % 4) * 4 + lane // 8 % 4)
    order = jnp.where(
        target == lax.broadcasted_iota(jnp.int32, (128, 128), 1), 1.0, 0.0).astype(BF16)
    results = []
    for p in range(4):
        pltpu.make_async_copy(zrecv.at[p], zrecv.at[p], zrecv_sem.at[p]).wait()
        results.append(zsend[p, z] + zrecv[p, 0] + zrecv[p, 1] + zrecv[p, 2])
    result = jnp.concatenate(results, axis=0)
    moved = jnp.dot(jnp.concatenate(split3(result), axis=0), order, preferred_element_type=F32)
    result = moved[:BLOCK] + moved[BLOCK:2 * BLOCK] + moved[2 * BLOCK:]
    other = pltpu.roll(result, 64, 1)
    for p, v in enumerate(PARTS):
        o_v[0, pl.ds(v, ROWS, stride=4), :] = result[p * ROWS:(p + 1) * ROWS]
        o_v[1, pl.ds(v, ROWS, stride=4), :] = other[p * ROWS:(p + 1) * ROWS]
    o_ref[...] = o_v[:, :, :N // (X * Z)]

    for p in range(4):
        if p == 0:
            most = rbuf.at[0, pl.ds(0, SCAN - 1)]
            pltpu.make_async_copy(most, most, send_sem.at[6]).wait()
        pltpu.make_async_copy(precv.at[p], precv.at[p], psend_sem.at[p]).wait()
        pltpu.make_async_copy(zrecv.at[p], zrecv.at[p], zsend_sem.at[p]).wait()


def local(even, odd, row, twiddle, intensities, trotter_labels, phase_shift):
    any_spec = pl.BlockSpec(memory_space=pl.ANY)
    dma = pltpu.SemaphoreType.DMA
    return pl.pallas_call(
        kernel,
        out_shape=jax.ShapeDtypeStruct((2, BLOCK, N // (X * Z)), F32),
        in_specs=[any_spec] * 7,
        out_specs=pl.BlockSpec(memory_space=pltpu.VMEM),
        scratch_shapes=[
            pltpu.VMEM((PIX, BLOCK, N), F32),
            pltpu.VMEM((8, PIX, BLOCK, 128), jnp.int32),
            pltpu.VMEM((8, BLOCK, 128), F32),
            pltpu.VMEM((2, 1024, 256), BF16),
            pltpu.VMEM((2, 1024, 512), BF16),
            pltpu.VMEM((2, 256, 256), BF16),
            pltpu.VMEM((2, 32, ROWS, 128), F32),
            pltpu.VMEM((N, 256), BF16),
            pltpu.VMEM((4, SCAN, 2, ROWS, 128), F32),
            pltpu.VMEM((4, SCAN, 2, ROWS, 128), F32),
            pltpu.VMEM((4, 8, 2, ROWS, 128), F32),
            pltpu.VMEM((256, 256), F32),
            pltpu.VMEM((2, 256, 256), BF16),
            pltpu.VMEM((8, BLOCK, 128), F32),
            pltpu.VMEM((8, BLOCK, 128), F32),
            pltpu.VMEM((4, 32, ROWS, 128), F32),
            pltpu.VMEM((4, 32, ROWS, 128), F32),
            pltpu.VMEM((4, X, 2, 2, ROWS, 128), F32),
            pltpu.VMEM((4, X - 1, 2, 2, ROWS, 128), F32),
            pltpu.VMEM((4, Z, ROWS, 128), F32),
            pltpu.VMEM((4, Z - 1, ROWS, 128), F32),
            pltpu.VMEM((2, BLOCK, 128), F32),
            dma((10,)),
            dma((7,)),
            dma((4,)),
            dma((4,)),
            dma((4,)),
            dma((4,)),
            dma((4,)),
        ],
        compiler_params=pltpu.CompilerParams(
            collective_id=0, has_side_effects=True, vmem_limit_bytes=55140 * 1024),
        name="ptycho",
    )(intensities, trotter_labels, phase_shift, even, odd, row, twiddle)


def solution(mesh):
    tables = make_tables()
    placed = (P("det", "scan", None), P("det", "scan", None), P("scan", None))
    fixed = tuple(P(*[None] * table.ndim) for table in tables)
    mapped = jax.shard_map(
        local, mesh=mesh, in_specs=fixed + placed, out_specs=P(None, "scan", "det"),
        check_vma=False)

    def run(intensities, trotter_labels, phase_shift):
        return mapped(*map(jnp.asarray, tables), intensities, trotter_labels, phase_shift)

    return run
```

```python
import math

import jax
import jax.numpy as jnp
import ml_dtypes
import numpy as np
from jax import lax
from jax.experimental import pallas as pl
from jax.experimental.pallas import tpu as pltpu
from jax.sharding import PartitionSpec as P

MESH = pl.DeviceIdType.MESH
F32 = jnp.float32
BF16 = jnp.bfloat16

N = 1024
SCAN = 32
BLOCK = 32
PARTS = (0, 2, 1, 3)
ROWS = BLOCK // 4
PIX = 4
X = 4
Z = 4
FIRST = 1


def split_table(table):
    high = table.astype(ml_dtypes.bfloat16)
    low = (table - high.astype(np.float64)).astype(ml_dtypes.bfloat16)
    return high, low


def make_tables():
    index = np.arange(N)
    angles = (index[:, None] * index[None, :] % N) * (2.0 * math.pi / N)
    cosine, sine = np.cos(angles), np.sin(angles)
    cos_v = cosine[:, :256].reshape(SCAN, ROWS, 4, 256)
    sin_v = sine[:, :256].reshape(SCAN, ROWS, 4, 256)
    even, odd = [], []
    for v in PARTS:
        c, s = cos_v[:, :, v], sin_v[:, :, v]
        if v % 2 == 0:
            table = np.stack([c, -s], axis=1)
        else:
            sign = 1.0 if v == 3 else -1.0
            table = np.stack(
                [np.concatenate([c, sign * s], 2), np.concatenate([-s, sign * c], 2)], axis=1)
        table = np.concatenate(split_table(table.reshape(512, -1)), axis=0)
        (odd if v % 2 else even).append(table)
    twiddle = np.stack([cosine[:32, :32], sine[:32, :32]])
    twiddle = np.tile(twiddle, (1, 1, PIX)).astype(np.float32)[:, :, None]
    twiddle = np.repeat(twiddle, ROWS, axis=2)
    u2 = np.arange(32)
    lanes = ((u2 % 4) * 32 + u2 // 4)[None, :] + 8 * np.arange(PIX)[:, None]
    small = np.zeros((2, 128, 128))
    for k in range(PIX):
        for e, table in enumerate((cosine, sine)):
            small[e, k * 32:(k + 1) * 32, lanes[k]] = table[:32, 0:N:32].T
    row = np.block([[small[0], -small[1]], [small[1], small[0]]]) / (N * 8.0)
    row = np.stack(split_table(row))
    return np.stack(even), np.stack(odd), row, twiddle


def swap_bit(first, second, width):
    clear = lax.broadcasted_iota(jnp.int32, first.shape, 1) % (2 * width) < width
    return (
        jnp.where(clear, first, pltpu.roll(second, width, 1)),
        jnp.where(clear, pltpu.roll(first, 128 - width, 1), second),
    )


def swap_bits(parts, widths):
    parts = list(parts)
    step = len(parts)
    for width in widths:
        step //= 2
        for n in range(len(parts)):
            if n // step % 2 == 0:
                parts[n], parts[n + step] = swap_bit(parts[n], parts[n + step], width)
    return parts


def sum_blocks(parts):
    lane = lax.broadcasted_iota(jnp.int32, parts[0].shape, 1)
    for width in (16, 8):
        clear = lane % (2 * width) < width
        half = len(parts) // 2
        sums = []
        for one, two in zip(parts[:half], parts[half:]):
            other = jnp.where(clear, two, one)
            other = jnp.where(
                clear, pltpu.roll(other, 128 - width, 1), pltpu.roll(other, width, 1))
            sums.append(jnp.where(clear, one, two) + other)
        parts = sums
    return parts[0]


def four_points(p):
    (ar, ai), (br, bi), (cr, ci), (dr, di) = p
    sr, si, er, ei = ar + cr, ai + ci, ar - cr, ai - ci
    tr, ti, fr, fi = br + dr, bi + di, br - dr, bi - di
    return [(sr + tr, si + ti), (er + fi, ei - fr), (sr - tr, si - ti), (er - fi, ei + fr)]


def eight_points(p):
    root = math.sqrt(0.5)
    even = four_points(p[0::2])
    odd = four_points(p[1::2])
    (r1, i1), (r2, i2), (r3, i3) = odd[1:]
    odd[1] = ((r1 + i1) * root, (i1 - r1) * root)
    odd[2] = (i2, -r2)
    odd[3] = ((i3 - r3) * root, -(r3 + i3) * root)
    out = [(e[0] + o[0], e[1] + o[1]) for e, o in zip(even, odd)]
    return out + [(e[0] - o[0], e[1] - o[1]) for e, o in zip(even, odd)]


def turn(p, step):
    if step == 0:
        return p
    c, s = math.cos(2.0 * math.pi * step / 32), math.sin(2.0 * math.pi * step / 32)
    return p[0] * c + p[1] * s, p[1] * c - p[0] * s


def split3(value):
    high = value.astype(BF16)
    rest = value - high.astype(F32)
    middle = rest.astype(BF16)
    return high, middle, (rest - middle.astype(F32)).astype(BF16)


def kernel(
    x_hbm, lab_hbm, phase_hbm, even_hbm, odd_hbm, row_hbm, twiddle_hbm, o_ref,
    x_v, lab_v, phase_v, even_v, odd_v, row_v, twiddle_v,
    xt, sbuf, rbuf, mixed, turned, lhs, cos_v, sin_v,
    wr, wi, psend, precv, zsend, zrecv, o_v,
    in_sem, send_sem, recv_sem, psend_sem, precv_sem, zsend_sem, zrecv_sem,
):
    me = lax.axis_index("scan")
    det = lax.axis_index("det")
    x, z = det // Z, det % Z

    x_copy = pltpu.make_async_copy(x_hbm, x_v, in_sem.at[0])
    lab_copies = [
        pltpu.make_async_copy(
            lab_hbm.at[:, :, pl.ds(m * 128, 128)], lab_v.at[m], in_sem.at[1])
        for m in range(8)
    ]
    phase_copies = [
        pltpu.make_async_copy(phase_hbm.at[:, pl.ds(m * 128, 128)], phase_v.at[m], in_sem.at[2])
        for m in range(8)
    ]
    row_copy = pltpu.make_async_copy(row_hbm, row_v, in_sem.at[3])
    twiddle_copy = pltpu.make_async_copy(twiddle_hbm, twiddle_v, in_sem.at[4])
    col_copies = [
        pltpu.make_async_copy(table.at[p % 2], to.at[p % 2], in_sem.at[6 + p])
        for p, (table, to) in enumerate([(even_hbm, even_v)] * 2 + [(odd_hbm, odd_v)] * 2)
    ]

    x_copy.start()
    col_copies[0].start()

    barrier = pltpu.get_barrier_semaphore()

    for i in range(1, SCAN):
        pl.semaphore_signal(
            barrier, inc=1, device_id=(lax.rem(me + i, SCAN), det), device_id_type=MESH)

    for i in range(1, 4):
        pl.semaphore_signal(
            barrier, inc=1, device_id=(me, lax.rem(x + i, X) * Z + z), device_id_type=MESH)
        pl.semaphore_signal(
            barrier, inc=1, device_id=(me, x * Z + lax.rem(z + i, Z)), device_id_type=MESH)

    for p in range(1, 4):
        col_copies[p].start()
    for copy in lab_copies + phase_copies:
        copy.start()
    row_copy.start()
    twiddle_copy.start()

    x_copy.wait()
    quarter = [[x_v[:, :, q * 256 + h * 128:q * 256 + (h + 1) * 128].reshape(128, 128)
                for q in range(4)] for h in range(2)]

    def put(value, at):
        value = jnp.transpose(value)
        high = value.astype(BF16)
        xt[at:at + 128, :128] = high
        xt[at:at + 128, 128:] = (value - high.astype(F32)).astype(BF16)

    for h, (x0, x1, x2, x3) in enumerate(quarter):
        put((x0 + x2) + (x1 + x3), h * 128)

    def column_part(p):
        col_copies[p].wait()
        table = even_v if p < 2 else odd_v
        rows = xt[p * 256:(p + 1) * 256] if p < 2 else xt[512:]
        prod = jnp.dot(table[p % 2], rows, preferred_element_type=F32)
        top = prod[:512] + prod[512:]
        sbuf[p] = (top[:, :128] + top[:, 128:]).reshape(SCAN, 2, ROWS, 128)

    chip, own = lax.div(me, 2), lax.rem(me, 2)

    def send(p, to, q):
        pltpu.make_async_remote_copy(
            src_ref=sbuf.at[p, to],
            dst_ref=rbuf.at[p, me],
            send_sem=send_sem.at[jnp.minimum(q, 6)],
            recv_sem=recv_sem.at[p],
            device_id=(to, det),
            device_id_type=MESH,
        ).start()

    def send_chunk(q):
        p, core = lax.div(q, 2), lax.rem(q, 2)

        @pl.when(jnp.logical_and(q == 6, me != FIRST))
        def _():
            send(p, FIRST, q)

        @pl.loop(1, 17)
        def _(i):
            to = lax.rem(chip + 8 * own + i, 16) * 2 + core
            led = jnp.logical_and(p == 3, to == FIRST)

            @pl.when(jnp.logical_not(jnp.logical_or(to == me, led)))
            def _():
                send(p, to, q)

    def wait_sent(q):
        same = lax.rem(q, 2) == own
        for mine, count in ((same, 15), (jnp.logical_not(same), 16)):
            @pl.when(mine)
            def _(count=count):
                most = rbuf.at[0, pl.ds(0, count)]
                pltpu.make_async_copy(most, most, send_sem.at[q]).wait()

    column_part(0)
    pl.semaphore_wait(barrier, SCAN - 1 + X - 1 + Z - 1)
    send_chunk(0)
    send_chunk(1)
    for h, (x0, x1, x2, x3) in enumerate(quarter):
        put((x0 + x2) - (x1 + x3), 256 + h * 128)
    column_part(1)
    send_chunk(2)
    send_chunk(3)
    for h, (x0, x1, x2, x3) in enumerate(quarter):
        put(x0 - x2, 512 + h * 128)
        put(x1 - x3, 768 + h * 128)
    column_part(2)
    column_part(3)
    for p in range(4):
        rbuf[p, me] = sbuf[p, me]

    pltpu.make_async_copy(phase_v, phase_v, in_sem.at[2]).wait()
    cos_v[...] = jnp.cos(phase_v[...])
    sin_v[...] = jnp.sin(phase_v[...])
    pltpu.make_async_copy(lab_v, lab_v, in_sem.at[1]).wait()
    for p, v in enumerate(PARTS):
        reals, imags = [], []
        for k in range(PIX):
            for m in range(8):
                cosine = cos_v[m, pl.ds(v, ROWS, stride=4), :]
                sine = sin_v[m, pl.ds(v, ROWS, stride=4), :]
                zero = jnp.zeros_like(cosine)
                labels = lab_v[m, k, pl.ds(v, ROWS, stride=4), :]
                left = labels == 1
                right = labels == 2
                reals.append(jnp.where(left, cosine, jnp.where(right, -cosine, zero)))
                imags.append(jnp.where(jnp.logical_or(left, right), -sine, zero))
        for to, parts in ((wr, reals), (wi, imags)):
            for u1, part in enumerate(swap_bits(parts, (16, 8, 4, 2, 1))):
                to[p, u1] = part

    row_copy.wait()
    twiddle_copy.wait()

    def row_part(p):
        most = rbuf.at[p, pl.ds(0, SCAN - 1)]
        pltpu.make_async_copy(most, most, recv_sem.at[p]).wait()
        for e in range(4):
            points = [(rbuf[p, 4 * g + e, 0], rbuf[p, 4 * g + e, 1]) for g in range(8)]
            for b, point in enumerate(eight_points(points)):
                mixed[e, b, 0], mixed[e, b, 1] = turn(point, e * b)
        for b in range(8):
            points = four_points([(mixed[e, b, 0], mixed[e, b, 1]) for e in range(4)])
            for c, (re, im) in enumerate(points):
                u1 = b + 8 * c
                cosine, sine = twiddle_v[0, u1], twiddle_v[1, u1]
                turned[u1 * ROWS:(u1 + 1) * ROWS, :128] = re * cosine + im * sine
                turned[u1 * ROWS:(u1 + 1) * ROWS, 128:] = im * cosine - re * sine
        for qh in range(2):
            value = turned[qh * 128:(qh + 1) * 128]
            high = value.astype(BF16)
            lhs[qh, :128] = high
            lhs[qh, 128:] = (value - high.astype(F32)).astype(BF16)
            both = jnp.dot(lhs[qh], row_v[0], preferred_element_type=F32)
            low = jnp.dot(lhs[qh, :128], row_v[1], preferred_element_type=F32)
            spec = both[:128] + both[128:] + low
            sums = [], []
            for ql in range(4):
                reals, imags = [], []
                for e in range(4):
                    at = ql * 4 + e
                    re = spec[at * ROWS:(at + 1) * ROWS, :128]
                    im = spec[at * ROWS:(at + 1) * ROWS, 128:]
                    w_re, w_im = wr[p, qh * 16 + at], wi[p, qh * 16 + at]
                    reals.append(re * w_re - im * w_im)
                    imags.append(re * w_im + im * w_re)
                sums[0].append(sum_blocks(reals))
                sums[1].append(sum_blocks(imags))
            for e in range(2):
                for q, part in enumerate(swap_bits(sums[e], (4, 2))):
                    psend[p, q, qh, e] = part

        @pl.loop(1, X)
        def _(j):
            q = (x + j) % X
            pltpu.make_async_remote_copy(
                src_ref=psend.at[p, q],
                dst_ref=precv.at[p, j - 1],
                send_sem=psend_sem.at[p],
                recv_sem=precv_sem.at[p],
                device_id=(me, q * Z + z),
                device_id_type=MESH,
            ).start()

    def sum_x(p):
        pltpu.make_async_copy(precv.at[p], precv.at[p], precv_sem.at[p]).wait()
        parts = []
        for qh in range(2):
            for e in range(2):
                total = psend[p, x, qh, e]
                for j in range(X - 1):
                    total = total + precv[p, j, qh, e]
                parts.append(total)
        for h, part in enumerate(swap_bits(parts, (1, 64))):
            zsend[p, h] = part

        @pl.loop(1, Z)
        def _(j):
            to = (z + j) % Z
            pltpu.make_async_remote_copy(
                src_ref=zsend.at[p, to],
                dst_ref=zrecv.at[p, j - 1],
                send_sem=zsend_sem.at[p],
                recv_sem=zrecv_sem.at[p],
                device_id=(me, x * Z + to),
                device_id_type=MESH,
            ).start()

    @pl.loop(0, 8)
    def _(q):
        p = lax.div(q, 2)

        @pl.when(q < 6)
        def _():
            wait_sent(q)

        @pl.when(jnp.logical_and(q > 1, q < 6))
        def _():
            send_chunk(q + 2)

        @pl.when(lax.rem(q, 2) == 1)
        def _():
            @pl.when(jnp.logical_and(p > 0, p < 3))
            def _():
                sum_x(p - 1)

            row_part(p)

    sum_x(2)
    sum_x(3)

    lane = lax.broadcasted_iota(jnp.int32, (128, 128), 0)
    target = (
        lane // 32 * 32 + (lane % 2 * 4 + lane // 2 % 4) * 4 + lane // 8 % 4)
    order = jnp.where(
        target == lax.broadcasted_iota(jnp.int32, (128, 128), 1), 1.0, 0.0).astype(BF16)
    results = []
    for p in range(4):
        pltpu.make_async_copy(zrecv.at[p], zrecv.at[p], zrecv_sem.at[p]).wait()
        results.append(zsend[p, z] + zrecv[p, 0] + zrecv[p, 1] + zrecv[p, 2])
    result = jnp.concatenate(results, axis=0)
    moved = jnp.dot(jnp.concatenate(split3(result), axis=0), order, preferred_element_type=F32)
    result = moved[:BLOCK] + moved[BLOCK:2 * BLOCK] + moved[2 * BLOCK:]
    other = pltpu.roll(result, 64, 1)
    for p, v in enumerate(PARTS):
        o_v[0, pl.ds(v, ROWS, stride=4), :] = result[p * ROWS:(p + 1) * ROWS]
        o_v[1, pl.ds(v, ROWS, stride=4), :] = other[p * ROWS:(p + 1) * ROWS]
    o_ref[...] = o_v[:, :, :N // (X * Z)]

    for p in range(4):
        if p == 0:
            most = rbuf.at[0, pl.ds(0, SCAN - 1)]
            pltpu.make_async_copy(most, most, send_sem.at[6]).wait()
        pltpu.make_async_copy(precv.at[p], precv.at[p], psend_sem.at[p]).wait()
        pltpu.make_async_copy(zrecv.at[p], zrecv.at[p], zsend_sem.at[p]).wait()


def local(even, odd, row, twiddle, intensities, trotter_labels, phase_shift):
    any_spec = pl.BlockSpec(memory_space=pl.ANY)
    dma = pltpu.SemaphoreType.DMA
    return pl.pallas_call(
        kernel,
        out_shape=jax.ShapeDtypeStruct((2, BLOCK, N // (X * Z)), F32),
        in_specs=[any_spec] * 7,
        out_specs=pl.BlockSpec(memory_space=pltpu.VMEM),
        scratch_shapes=[
            pltpu.VMEM((PIX, BLOCK, N), F32),
            pltpu.VMEM((8, PIX, BLOCK, 128), jnp.int32),
            pltpu.VMEM((8, BLOCK, 128), F32),
            pltpu.VMEM((2, 1024, 256), BF16),
            pltpu.VMEM((2, 1024, 512), BF16),
            pltpu.VMEM((2, 256, 256), BF16),
            pltpu.VMEM((2, 32, ROWS, 128), F32),
            pltpu.VMEM((N, 256), BF16),
            pltpu.VMEM((4, SCAN, 2, ROWS, 128), F32),
            pltpu.VMEM((4, SCAN, 2, ROWS, 128), F32),
            pltpu.VMEM((4, 8, 2, ROWS, 128), F32),
            pltpu.VMEM((256, 256), F32),
            pltpu.VMEM((2, 256, 256), BF16),
            pltpu.VMEM((8, BLOCK, 128), F32),
            pltpu.VMEM((8, BLOCK, 128), F32),
            pltpu.VMEM((4, 32, ROWS, 128), F32),
            pltpu.VMEM((4, 32, ROWS, 128), F32),
            pltpu.VMEM((4, X, 2, 2, ROWS, 128), F32),
            pltpu.VMEM((4, X - 1, 2, 2, ROWS, 128), F32),
            pltpu.VMEM((4, Z, ROWS, 128), F32),
            pltpu.VMEM((4, Z - 1, ROWS, 128), F32),
            pltpu.VMEM((2, BLOCK, 128), F32),
            dma((10,)),
            dma((7,)),
            dma((4,)),
            dma((4,)),
            dma((4,)),
            dma((4,)),
            dma((4,)),
        ],
        compiler_params=pltpu.CompilerParams(
            collective_id=0, has_side_effects=True, vmem_limit_bytes=55140 * 1024),
        name="ptycho",
    )(intensities, trotter_labels, phase_shift, even, odd, row, twiddle)


def solution(mesh):
    tables = make_tables()
    placed = (P("det", "scan", None), P("det", "scan", None), P("scan", None))
    fixed = tuple(P(*[None] * table.ndim) for table in tables)
    mapped = jax.shard_map(
        local, mesh=mesh, in_specs=fixed + placed, out_specs=P(None, "scan", "det"),
        check_vma=False)

    def run(intensities, trotter_labels, phase_shift):
        return mapped(*map(jnp.asarray, tables), intensities, trotter_labels, phase_shift)

    return run
```
